32 devices in a mesh: kmer: 8 (over z, y), samp: 4 (over x, core).
Axes of the slice: x: 2, y: 2, z: 4, core: 2. Of those that a mesh axis runs over, the one named last changes fastest.
Arguments:
- abundance: float32 [16384, 4096], P('kmer', 'samp'), may hold values from 1 to 100
- loadings: float32 [16384, 256], P('kmer', 'samp'), may hold values from 0.01 to 5, as said below
- activity: float32 [256, 4096], P('kmer', 'samp'), may hold values from 0.01 to 5, as said below
Outputs:
- new_loadings: float32 [16384, 256], P('kmer', 'samp')
- new_activity: float32 [256, 4096], P('kmer', 'samp')
The draws below stay inside these ranges and needn't reach their ends.
Inputs may be any that keep to these rules, and one draw needn't show every extreme that they name: `loadings`: positive entries. `activity`: positive entries.
All inputs are finite; a program needn't handle non-finite values.
Results may differ from the reference program's by a relative error of at most 0.0001.
Values sent between devices are 32-bit elements; how exact they have to be, the bound alone decides.
A program may use at most 64 MiB of HBM per device.

```python
import math
import jax
import jax.numpy as jnp
from jax import lax

K = 256
MD = 2048
M = 16384
N = 4096
N_KMER = 8


def draw_loadings(key, part):
    first = jax.random.fold_in(jax.random.fold_in(key, 11), 0)
    rising = 1.0 + 2.0 * jnp.arange(M, dtype=jnp.float32)[:, None] / (M - 1)
    base = jnp.exp(jax.random.uniform(first, (M, K), jnp.float32, jnp.log(0.05), jnp.log(0.5)))
    return base * rising


def draw_activity(key, part):
    first = jax.random.fold_in(jax.random.fold_in(key, 23), 0)
    third = jax.random.fold_in(jax.random.fold_in(key, 23), 2)
    position = jnp.arange(N, dtype=jnp.float32)[None, :] / (N - 1)
    rising = 1.0 + 2.0 * position
    slopes = jax.random.uniform(third, (K, 1), jnp.float32, -1.0, 1.0)
    profile = jnp.exp(slopes * (2.0 * position - 1.0))
    base = jnp.exp(jax.random.uniform(first, (K, N), jnp.float32, jnp.log(0.05), jnp.log(0.5)))
    return base * rising * profile


def steps_of(stream_key, extent, cuts, smallest, high):
    loudness, own = 1.0, jax.random.fold_in(stream_key, 6)
    for axis_at, shards_of in cuts:
        draws = jnp.exp(jax.random.uniform(jax.random.fold_in(own, axis_at), (shards_of,), jnp.float32, smallest / len(cuts), high / len(cuts)))
        loudness = loudness * jnp.repeat(draws, extent[axis_at] // shards_of).reshape([-1 if axis == axis_at else 1 for axis in range(len(extent))])
    return loudness


def setup_inputs(seed: int = 0) -> dict:
    key_of = jax.random.split(jax.random.key(seed), 4)
    abundance = jnp.clip(jnp.exp(math.log(100.0) - 4.6051702 * jax.random.uniform(key_of[0], (M, N), jnp.float32) ** steps_of(key_of[0], (M, N), ((0, 8), (1, 4)), -0.2, 0.2)), 1.0, 100.0)
    loadings = draw_loadings(jax.random.fold_in(key_of[3], 71), 0)
    activity = draw_activity(jax.random.fold_in(key_of[3], 71), 0)
    return {"abundance": abundance, "loadings": loadings, "activity": activity}


def reference(abundance, loadings, activity):
    highest = lax.Precision.HIGHEST
    activity_sums = jnp.sum(activity, axis=1)
    data_blocks = abundance.reshape(N_KMER, MD, N)
    load_blocks = loadings.reshape(N_KMER, MD, K)

    def update_rows(block_pair):
        data_block, load_block = block_pair
        rebuilt = jnp.dot(load_block, activity, precision=highest, preferred_element_type=jnp.float32)
        quotient = data_block / rebuilt
        numer = jnp.dot(quotient, activity.T, precision=highest, preferred_element_type=jnp.float32)
        return load_block * numer / activity_sums

    new_blocks = lax.map(update_rows, (data_blocks, load_blocks))
    new_loadings = new_blocks.reshape(N_KMER * MD, K)
    loading_sums = jnp.sum(new_loadings, axis=0)

    def accumulate(total, block_pair):
        data_block, load_block = block_pair
        rebuilt = jnp.dot(load_block, activity, precision=highest, preferred_element_type=jnp.float32)
        quotient = data_block / rebuilt
        return total + jnp.dot(load_block.T, quotient, precision=highest, preferred_element_type=jnp.float32), None

    numer_h, _ = lax.scan(accumulate, jnp.zeros((K, N), jnp.float32), (data_blocks, new_blocks))
    new_activity = activity * numer_h / loading_sums[:, None]
    return new_loadings, new_activity
```

```python
import functools

import jax
import jax.numpy as jnp
from jax import lax
from jax.experimental import pallas as pl
from jax.experimental.pallas import tpu as pltpu
from jax.sharding import PartitionSpec as P

F32, BF16 = jnp.float32, jnp.bfloat16
LANES = 128
CORES = 2


def halves(value):
    high = value.astype(BF16)
    return high, (value - high.astype(F32)).astype(BF16)


def quotient_of(above, below):
    guess = pl.reciprocal(below, approx=True)
    return above * (guess * (2.0 - below * guess))


def dot(a, b):
    return jnp.dot(a, b, preferred_element_type=F32)


def kernel(
    sizes, ab_hbm, load_ref, act_ref, newload_ref, newact_ref,
    ab, wbuf, wfull, w3, hbuf, h3, ht3, tbuf, nbuf, recv_a, sbuf, recv_x, ubuf, acc, recv_y, ybuf, recv_z,
    ab_sem, hz_s, hy_s, h_r, wx_s, wc_s, wf_s, w_r, t_s, t_r, a_s, a_r, x_s, x_r, u_s, u_r, ry_s, ry_r, rz_s, rz_r,
):
    n_k, n_s, n_z, n_y, chunk = sizes
    n_x = n_s // CORES
    rows_m, width = load_ref.shape
    rows_h, cols = act_ref.shape
    rank = rows_h * n_k
    per_tile = LANES // width
    packed = rows_m // per_tile
    pieces = packed // chunk
    chunks = rows_m // chunk
    half = chunk // 2

    k, s = lax.axis_index("kmer"), lax.axis_index("samp")
    z, y = lax.div(k, n_y), lax.rem(k, n_y)
    x, core = lax.div(s, CORES), lax.rem(s, CORES)
    mate = x * CORES + (1 - core)

    def z_at(d):
        return lax.rem(z + d, n_z)

    def y_at(d):
        return lax.rem(y + d, n_y)

    def x_at(d):
        return lax.rem(x + d, n_x) * CORES + core

    def put(src, dst, send, recv, kk, ss):
        return pltpu.make_async_remote_copy(
            src_ref=src, dst_ref=dst, send_sem=send, recv_sem=recv,
            device_id={"kmer": kk, "samp": ss}, device_id_type=pl.DeviceIdType.MESH,
        )

    def block(start, size):
        return pl.ds(pl.multiple_of(start, size), size)

    def arrived(dst, sem):
        put(dst, dst, sem, sem, k, mate).wait_recv()

    sent = []

    def go(*args):
        copy = put(*args)
        copy.start()
        sent.append(copy)

    fetch = pltpu.make_async_copy(ab_hbm, ab, ab_sem)
    fetch.start()

    hbuf[block(k * rows_h, rows_h), :] = act_ref[...]
    wbuf[s] = jnp.concatenate([load_ref[q * packed:(q + 1) * packed, :] for q in range(per_tile)], axis=1)

    barrier = pltpu.get_barrier_semaphore()
    peers = [(z_at(d) * n_y + y, s) for d in range(1, n_z)]
    peers += [(z * n_y + y_at(d), s) for d in range(1, n_y)]
    peers += [(k, lax.rem(s + d, n_s)) for d in range(1, n_s)]
    for kk, ss in peers:
        pl.semaphore_signal(
            barrier, inc=1, device_id={"kmer": kk, "samp": ss}, device_id_type=pl.DeviceIdType.MESH
        )
    pl.semaphore_wait(barrier, len(peers))

    near = []
    for d in range(1, n_z // 2 + 1):
        near += [d] if d == n_z - d else [d, n_z - d]

    def hslot(kk):
        return hbuf.at[block(kk * rows_h, rows_h), :]

    def wslot(ss, j):
        return wbuf.at[ss, pl.ds(j * chunk, chunk), :]

    def pass_y(i, zz):
        slot = hslot(zz * n_y + y)
        for d in range(1, n_y):
            go(slot, slot, hy_s.at[i, d - 1], h_r.at[zz * n_y + y], z * n_y + y_at(d), s)

    for i, d in enumerate(near):
        go(hslot(k), hslot(k), hz_s.at[i], h_r.at[k], z_at(d) * n_y + y, s)
        if i == 0:
            pass_y(0, z)
    for j in range(pieces):
        for d in range(1, n_x):
            go(wslot(s, j), wslot(s, j), wx_s.at[d - 1, j], w_r.at[s, j], k, x_at(d))
        go(wslot(s, j), wslot(s, j), wc_s.at[j], w_r.at[s, j], k, mate)

    def take_h(i):
        src = lax.rem(z + n_z - near[i], n_z)
        arrived(hslot(src * n_y + y), h_r.at[src * n_y + y])
        pass_y(i + 1, src)

    def take_w(j):
        for d in range(1, n_x):
            src = x_at(d)
            arrived(wslot(src, j), w_r.at[src, j])
            go(wslot(src, j), wslot(src, j), wf_s.at[d - 1, j], w_r.at[src, j], k, mate)

    for i in range(max(len(near), pieces)):
        if i < len(near):
            take_h(i)
        if i < pieces:
            take_w(i)

    for j in range(pieces):
        for d in range(n_x):
            src = lax.rem(x + d, n_x) * CORES + (1 - core)
            arrived(wslot(src, j), w_r.at[src, j])
        for q in range(per_tile):
            at = q * packed + j * chunk
            whole = jnp.concatenate(
                [wbuf[i, j * chunk:(j + 1) * chunk, q * width:(q + 1) * width] for i in range(n_s)], axis=1
            )
            wfull[at:at + chunk, :] = whole
            high, low = halves(whole)
            w3[at:at + chunk, :] = jnp.concatenate([high, high, low], axis=1)

    for d in range(1, n_y):
        for i in range(n_z):
            src = i * n_y + y_at(d)
            arrived(hslot(src), h_r.at[src])

    high, low = halves(hbuf[...])
    h3[...] = jnp.concatenate([high, low, high], axis=0)
    turned = hbuf[...].T
    high, low = halves(turned)
    ht3[...] = jnp.concatenate([high, low, high], axis=0)
    tbuf[s] = jnp.broadcast_to(jnp.sum(turned, axis=0, keepdims=True), (8, rank))
    for d in range(1, n_s):
        go(tbuf.at[s], tbuf.at[s], t_s.at[d - 1], t_r.at[s], k, lax.rem(s + d, n_s))
    fetch.wait()

    def out_a(c):
        return put(
            nbuf.at[block(c * chunk + (1 - core) * half, half), :], recv_a.at[block(c * half, half), :],
            a_s.at[c], a_r.at[c], k, mate,
        )

    def out_x(c, d):
        rows = block(c * half, half)
        return put(sbuf.at[rows, :], recv_x.at[d - 1, rows, :], x_s.at[d - 1, c], x_r.at[d - 1, c], k, x_at(d))

    def out_u(c):
        rows = block(c * chunk + core * half, half)
        return put(ubuf.at[rows, :], ubuf.at[rows, :], u_s.at[c], u_r.at[c], k, mate)

    def rows_step(c, carry):
        @pl.when(c < chunks)
        def _():
            rows = block(c * chunk, chunk)
            quotient = quotient_of(ab[rows, :], dot(w3[rows, :], h3[...]))
            high, low = halves(quotient)
            nbuf[rows, :] = dot(jnp.concatenate([high, high, low], axis=1), ht3[...])
            out_a(c).start()

        @pl.when(c >= 1)
        def _():
            b = c - 1
            out_a(b).wait_recv()
            rows = block(b * half, half)
            sbuf[rows, :] = nbuf[block(b * chunk + core * half, half), :] + recv_a[rows, :]
            for d in range(1, n_x):
                out_x(b, d).start()

        return carry

    lax.fori_loop(0, chunks + 1, rows_step, 0)

    for d in range(1, n_s):
        src = lax.rem(s + d, n_s)
        arrived(tbuf.at[src], t_r.at[src])
    totals = tbuf[0, 0:1, :]
    for i in range(1, n_s):
        totals = totals + tbuf[i, 0:1, :]
    scale = 1.0 / totals
    acc[...] = jnp.zeros_like(acc)

    def cols_step(c, carry):
        @pl.when(c < chunks)
        def _():
            rows = block(c * half, half)
            total = sbuf[rows, :]
            for d in range(1, n_x):
                out_x(c, d).wait_recv()
                total = total + recv_x[d - 1, rows, :]
            mine = block(c * chunk + core * half, half)
            ubuf[mine, :] = wfull[mine, :] * total * scale
            out_u(c).start()

        @pl.when(c >= 1)
        def _():
            b = c - 1
            out_u(b).wait_recv()
            rows = block(b * chunk, chunk)
            updated = ubuf[rows, :]
            high, low = halves(updated)
            rebuilt = dot(jnp.concatenate([high, high, low], axis=1), h3[...])
            q_high, q_low = halves(quotient_of(ab[rows, :], rebuilt))
            turned = updated.T
            high, low = halves(turned)
            acc[:, :cols] += dot(
                jnp.concatenate([high, high, low], axis=1), jnp.concatenate([q_high, q_low, q_high], axis=0)
            )
            acc[:, cols:] += jnp.broadcast_to(jnp.sum(turned, axis=1, keepdims=True), (rank, LANES))

        return carry

    lax.fori_loop(0, chunks + 1, cols_step, 0)

    far = near[::-1] + [0]
    for i, d in enumerate(far):
        for e in range(1, n_y):
            go(
                acc.at[block((z_at(d) * n_y + y_at(e)) * rows_h, rows_h), :], recv_y.at[e - 1, i],
                ry_s.at[e - 1, i], ry_r.at[e - 1, i], z * n_y + y_at(e), s,
            )

    for i in range(n_s):
        @pl.when(s == i)
        def _():
            newload_ref[...] = ubuf[:, i * width:(i + 1) * width]

    total = None
    for i, d in enumerate(far):
        total = acc[block((z_at(d) * n_y + y) * rows_h, rows_h), :]
        for e in range(1, n_y):
            arrived(recv_y.at[e - 1, i], ry_r.at[e - 1, i])
            total = total + recv_y[e - 1, i]
        if d:
            ybuf[i] = total
            go(ybuf.at[i], recv_z.at[i], rz_s.at[i], rz_r.at[i], z_at(d) * n_y + y, s)
    for i in range(n_z - 1):
        arrived(recv_z.at[i], rz_r.at[i])
        total = total + recv_z[i]
    newact_ref[...] = act_ref[...] * total[:, :cols] / total[:, cols:cols + 1]

    for copy in sent:
        copy.wait_send()

    def close(c, carry):
        out_a(c).wait_send()
        out_u(c).wait_send()
        for d in range(1, n_x):
            out_x(c, d).wait_send()
        return carry

    lax.fori_loop(0, chunks, close, 0)


def solution(mesh):
    n_k, n_s = mesh.shape["kmer"], mesh.shape["samp"]
    n_y = max(d for d in range(1, n_k + 1) if n_k % d == 0 and d * d <= n_k)
    n_z, n_x = n_k // n_y, n_s // CORES

    def per_device(abundance, loadings, activity):
        rows_m, width = loadings.shape
        rows_h, cols = activity.shape
        rank = rows_h * n_k
        packed = rows_m * width // LANES
        chunk = min(256, packed)
        chunks, pieces = rows_m // chunk, packed // chunk
        vmem, dma = pltpu.VMEM, pltpu.SemaphoreType.DMA
        whole = pl.BlockSpec(memory_space=pltpu.VMEM)
        return pl.pallas_call(
            functools.partial(kernel, (n_k, n_s, n_z, n_y, chunk)),
            out_shape=(
                jax.ShapeDtypeStruct((rows_m, width), F32),
                jax.ShapeDtypeStruct((rows_h, cols), F32),
            ),
            in_specs=[pl.BlockSpec(memory_space=pl.ANY), whole, whole],
            out_specs=(whole, whole),
            scratch_shapes=[
                vmem((rows_m, cols), F32),
                vmem((n_s, packed, LANES), F32),
                vmem((rows_m, rank), F32),
                vmem((rows_m, 3 * rank), BF16),
                vmem((rank, cols), F32),
                vmem((3 * rank, cols), BF16),
                vmem((3 * cols, rank), BF16),
                vmem((n_s, 8, rank), F32),
                vmem((rows_m, rank), F32),
                vmem((rows_m // 2, rank), F32),
                vmem((rows_m // 2, rank), F32),
                vmem((n_x - 1, rows_m // 2, rank), F32),
                vmem((rows_m, rank), F32),
                vmem((rank, cols + LANES), F32),
                vmem((n_y - 1, n_z, rows_h, cols + LANES), F32),
                vmem((n_z - 1, rows_h, cols + LANES), F32),
                vmem((n_z - 1, rows_h, cols + LANES), F32),
                dma,
                dma((n_z - 1,)),
                dma((n_z, n_y - 1)),
                dma((n_k,)),
                dma((n_x - 1, pieces)),
                dma((pieces,)),
                dma((n_x - 1, pieces)),
                dma((n_s, pieces)),
                dma((n_s - 1,)),
                dma((n_s,)),
                dma((chunks,)),
                dma((chunks,)),
                dma((n_x - 1, chunks)),
                dma((n_x - 1, chunks)),
                dma((chunks,)),
                dma((chunks,)),
                dma((n_y - 1, n_z)),
                dma((n_y - 1, n_z)),
                dma((n_z - 1,)),
                dma((n_z - 1,)),
            ],
            compiler_params=pltpu.CompilerParams(
                collective_id=0, has_side_effects=True, vmem_limit_bytes=56 * 2**20
            ),
            cost_estimate=pl.CostEstimate(
                flops=24 * rows_m * cols * rank,
                bytes_accessed=4 * rows_m * cols,
                transcendentals=2 * rows_m * cols,
            ),
        )(abundance, loadings, activity)

    in_specs = (P("kmer", "samp"), P("kmer", "samp"), P("kmer", "samp"))
    out_specs = (P("kmer", "samp"), P("kmer", "samp"))
    return jax.shard_map(
        per_device, mesh=mesh, in_specs=in_specs, out_specs=out_specs, check_vma=False
    )
```

```python
import functools

import jax
import jax.numpy as jnp
from jax import lax
from jax.experimental import pallas as pl
from jax.experimental.pallas import tpu as pltpu
from jax.sharding import PartitionSpec as P

F32, BF16 = jnp.float32, jnp.bfloat16
LANES = 128
PIECE = 512
PARTS = 2
FLYING = 3
CORES = 2


def halves(value):
    high = value.astype(BF16)
    return high, (value - high.astype(F32)).astype(BF16)


def quotient_of(above, below):
    guess = pl.reciprocal(below, approx=True)
    return above * (guess * (2.0 - below * guess))


def dot(a, b):
    return jnp.dot(a, b, preferred_element_type=F32)


def kernel(
    sizes, ab_hbm, load_ref, act_ref, newload_ref, newact_ref,
    ab, wbuf, wfull, w3, hbuf, h3, ht3, tbuf, tsum, nbuf, recv_a, sbuf, recv_x, ubuf, uturn, acc, cbuf, csum, recv_y, ybuf, recv_z,
    ab_sem, hr_s, hl_s, hy_s, h_r, wx_s, wc_s, wf_s, w_r, t_s, t_r, a_s, a_r, x_s, x_r, u_s, u_r, c_s, c_r,
    ry_s, ry_r, rz_s, rz_r,
):
    n_k, n_s, n_z, n_y, chunk = sizes
    n_x = n_s // CORES
    width, rows_m = load_ref.shape
    rows_h, cols = act_ref.shape
    rank = rows_h * n_k
    pieces = rows_m // PIECE
    chunks = rows_m // chunk
    half = chunk // 2

    k, s = lax.axis_index("kmer"), lax.axis_index("samp")
    z, y = lax.div(k, n_y), lax.rem(k, n_y)
    x, core = lax.div(s, CORES), lax.rem(s, CORES)
    mate = x * CORES + (1 - core)

    def z_at(d):
        return lax.rem(z + d, n_z)

    def y_at(d):
        return lax.rem(y + d, n_y)

    def x_at(d):
        return lax.rem(x + d, n_x) * CORES + core

    def put(src, dst, send, recv, kk, ss):
        return pltpu.make_async_remote_copy(
            src_ref=src, dst_ref=dst, send_sem=send, recv_sem=recv,
            device_id={"kmer": kk, "samp": ss}, device_id_type=pl.DeviceIdType.MESH,
        )

    def block(start, size):
        return pl.ds(pl.multiple_of(start, size), size)

    def arrived(dst, sem):
        put(dst, dst, sem, sem, k, mate).wait_recv()

    sent = []

    def go(*args, when=None):
        copy = put(*args)
        sent.append((when, copy))
        if when is None:
            copy.start()
        else:
            pl.when(when)(copy.start)

    fetch = pltpu.make_async_copy(ab_hbm, ab, ab_sem)
    fetch.start()

    hbuf[block(k * rows_h, rows_h), :] = act_ref[...]
    wbuf[block(s * width, width), :] = load_ref[...]

    barrier = pltpu.get_barrier_semaphore()
    peers = [(lax.rem(k + d, n_k), s) for d in range(1, n_k)]
    peers += [(k, lax.rem(s + d, n_s)) for d in range(1, n_s)]
    for kk, ss in peers:
        pl.semaphore_signal(
            barrier, inc=1, device_id={"kmer": kk, "samp": ss}, device_id_type=pl.DeviceIdType.MESH
        )
    pl.semaphore_wait(barrier, len(peers))

    def hslot(kk):
        return hbuf.at[block(kk * rows_h, rows_h), :]

    def wslot(ss, j):
        return wbuf.at[block(ss * width, width), pl.ds(j * PIECE, PIECE)]

    def pass_h(zz, i, when):
        kk = zz * n_y + y
        slot = hslot(kk)
        up, down = jnp.minimum(z + 1, n_z - 1), jnp.maximum(z - 1, 0)
        if i >= 0:
            ok = z < n_z - 1
            go(slot, slot, hr_s.at[abs(i)], h_r.at[kk], up * n_y + y, s, when=ok if when is None else ok & when)
        if i <= 0:
            ok = z > 0
            go(slot, slot, hl_s.at[abs(i)], h_r.at[kk], down * n_y + y, s, when=ok if when is None else ok & when)
        for d in range(1, n_y):
            go(slot, slot, hy_s.at[n_z - 1 + i, d - 1], h_r.at[kk], z * n_y + y_at(d), s, when=when)

    pass_h(z, 0, None)
    for j in range(pieces):
        for d in range(1, n_x):
            go(wslot(s, j), wslot(s, j), wx_s.at[d - 1, j], w_r.at[s, j], k, x_at(d))
        go(wslot(s, j), wslot(s, j), wc_s.at[j], w_r.at[s, j], k, mate)

    def take_h(i):
        there = (z >= i) if i > 0 else (z - i <= n_z - 1)
        zz = jnp.clip(z - i, 0, n_z - 1)
        kk = zz * n_y + y

        @pl.when(there)
        def _():
            arrived(hslot(kk), h_r.at[kk])

        pass_h(zz, i, there)

    def take_w(j):
        for d in range(1, n_x):
            src = x_at(d)
            arrived(wslot(src, j), w_r.at[src, j])
            go(wslot(src, j), wslot(src, j), wf_s.at[d - 1, j], w_r.at[src, j], k, mate)

    for i in range(max(n_z - 1, pieces)):
        if i < n_z - 1:
            take_h(i + 1)
            take_h(-i - 1)
        if i < pieces:
            take_w(i)

    for j in range(pieces):
        for d in range(n_x):
            src = lax.rem(x + d, n_x) * CORES + (1 - core)
            arrived(wslot(src, j), w_r.at[src, j])
        for at in range(j * PIECE, (j + 1) * PIECE, chunk):
            whole = wbuf[:, at:at + chunk].T
            wfull[at:at + chunk, :] = whole
            high, low = halves(whole)
            w3[at:at + chunk, :] = jnp.concatenate([high, high, low], axis=1)

    for d in range(1, n_y):
        for i in range(n_z):
            src = i * n_y + y_at(d)
            arrived(hslot(src), h_r.at[src])

    high, low = halves(hbuf[...])
    h3[...] = jnp.concatenate([high, low, high], axis=0)
    turned = hbuf[...].T
    high, low = halves(turned)
    ht3[...] = jnp.concatenate([high, low, high], axis=0)
    tbuf[s] = jnp.broadcast_to(jnp.sum(turned, axis=0, keepdims=True), (8, rank))
    for d in range(1, n_s):
        go(tbuf.at[s], tbuf.at[s], t_s.at[d - 1], t_r.at[s], k, lax.rem(s + d, n_s))
    fetch.wait()

    def out_a(c):
        return put(
            nbuf.at[block(c * chunk + (1 - core) * half, half), :], recv_a.at[block(c * half, half), :],
            a_s.at[c], a_r.at[c], k, mate,
        )

    def out_x(c, d):
        rows = block(c * half, half)
        return put(sbuf.at[rows, :], recv_x.at[d - 1, rows, :], x_s.at[d - 1, c], x_r.at[d - 1, c], k, x_at(d))

    def out_u(c):
        rows = block(c * chunk + core * half, half)
        return put(ubuf.at[rows, :], ubuf.at[rows, :], u_s.at[c], u_r.at[c], k, mate)

    ahead = max(1, chunks // 2)

    def scale_rows(c):
        rows = block(c * half, half)
        total = sbuf[rows, :]
        for d in range(1, n_x):
            out_x(c, d).wait_recv()
            total = total + recv_x[d - 1, rows, :]
        mine = block(c * chunk + core * half, half)
        ubuf[mine, :] = wfull[mine, :] * total * tsum[0:1, :]
        out_u(c).start()

    def rows_step(c, carry):
        @pl.when(c < chunks)
        def _():
            rows = block(c * chunk, chunk)
            quotient = quotient_of(ab[rows, :], dot(w3[rows, :], h3[...]))
            high, low = halves(quotient)
            nbuf[rows, :] = dot(jnp.concatenate([high, high, low], axis=1), ht3[...])
            out_a(c).start()

        @pl.when(c == 1)
        def _():
            for d in range(1, n_s):
                src = lax.rem(s + d, n_s)
                arrived(tbuf.at[src], t_r.at[src])
            totals = tbuf[0]
            for i in range(1, n_s):
                totals = totals + tbuf[i]
            tsum[...] = 1.0 / totals

        @pl.when(c != 1)
        def _():
            b = jnp.maximum(c - 1, 0)
            out_a(b).wait_recv()
            rows = block(b * half, half)
            sbuf[rows, :] = nbuf[block(b * chunk + core * half, half), :] + recv_a[rows, :]
            for d in range(1, n_x):
                out_x(b, d).start()

        @pl.when(c > ahead)
        def _():
            scale_rows(c - 1 - ahead)

        return carry

    lax.fori_loop(0, chunks + 1, rows_step, 0)
    acc[...] = jnp.zeros_like(acc)
    csum[...] = jnp.zeros_like(csum)

    def cols_step(c, carry):
        @pl.when((c < chunks) & (c >= chunks - ahead))
        def _():
            scale_rows(c)

        @pl.when(c >= 1)
        def _():
            b = c - 1
            out_u(b).wait_recv()
            rows = block(b * chunk, chunk)
            updated = ubuf[rows, :]
            csum[...] += jnp.broadcast_to(jnp.sum(updated, axis=0, keepdims=True), csum.shape)
            high, low = halves(updated)
            rebuilt = dot(jnp.concatenate([high, high, low], axis=1), h3[...])
            q_high, q_low = halves(quotient_of(ab[rows, :], rebuilt))
            turned = updated.T
            uturn[:, rows] = turned
            high, low = halves(turned)
            acc[...] += dot(
                jnp.concatenate([high, high, low], axis=1), jnp.concatenate([q_high, q_low, q_high], axis=0)
            )

        return carry

    lax.fori_loop(0, chunks + 1, cols_step, 0)

    near = []
    for d in range(1, n_z // 2 + 1):
        near += [d] if d == n_z - d else [d, n_z - d]
    part = cols // PARTS
    steps = [(i, d, p) for i, d in enumerate(near[::-1] + [0]) for p in range(PARTS)]

    def part_of(p):
        return pl.ds(p * part, part)

    def send_y(i, d, p):
        for e in range(1, n_y):
            go(
                acc.at[block((z_at(d) * n_y + y_at(e)) * rows_h, rows_h), part_of(p)],
                recv_y.at[e - 1, i, :, part_of(p)],
                ry_s.at[e - 1, i, p], ry_r.at[e - 1, i, p], z * n_y + y_at(e), s,
            )

    for step in steps[:FLYING]:
        send_y(*step)
    cbuf[k] = csum[...]
    for d in range(1, n_k):
        go(cbuf.at[k], cbuf.at[k], c_s.at[d - 1], c_r.at[k], lax.rem(k + d, n_k), s)
    newload_ref[...] = uturn[block(s * width, width), :]

    for at, (i, d, p) in enumerate(steps):
        for e in range(1, n_y):
            arrived(recv_y.at[e - 1, i, :, part_of(p)], ry_r.at[e - 1, i, p])
        if at + FLYING < len(steps):
            send_y(*steps[at + FLYING])
        total = acc[block((z_at(d) * n_y + y) * rows_h, rows_h), part_of(p)]
        for e in range(1, n_y):
            total = total + recv_y[e - 1, i, :, part_of(p)]
        ybuf[i, :, part_of(p)] = total
        if d:
            go(
                ybuf.at[i, :, part_of(p)], recv_z.at[i, :, part_of(p)],
                rz_s.at[i, p], rz_r.at[i, p], z_at(d) * n_y + y, s,
            )

    for d in range(1, n_k):
        src = lax.rem(k + d, n_k)
        arrived(cbuf.at[src], c_r.at[src])
    sums = cbuf[0, 0:1, :]
    for i in range(1, n_k):
        sums = sums + cbuf[i, 0:1, :]
    uturn[:, 0:LANES] = jnp.broadcast_to(sums, (LANES, rank)).T
    scaled = act_ref[...] / uturn[block(k * rows_h, rows_h), 0:1]
    for p in range(PARTS):
        total = ybuf[n_z - 1, :, part_of(p)]
        for i in range(n_z - 1):
            arrived(recv_z.at[i, :, part_of(p)], rz_r.at[i, p])
            total = total + recv_z[i, :, part_of(p)]
        newact_ref[:, part_of(p)] = scaled[:, p * part:(p + 1) * part] * total

    for when, copy in sent:
        if when is None:
            copy.wait_send()
        else:
            pl.when(when)(copy.wait_send)

    def close(c, carry):
        out_a(c).wait_send()
        out_u(c).wait_send()
        for d in range(1, n_x):
            out_x(c, d).wait_send()
        return carry

    lax.fori_loop(0, chunks, close, 0)


def solution(mesh):
    n_k, n_s = mesh.shape["kmer"], mesh.shape["samp"]
    n_y = max(d for d in range(1, n_k + 1) if n_k % d == 0 and d * d <= n_k)
    n_z, n_x = n_k // n_y, n_s // CORES

    def per_device(abundance, loadings, activity):
        rows_m, width = loadings.shape
        rows_h, cols = activity.shape
        rank = rows_h * n_k
        chunk = 256
        chunks, pieces = rows_m // chunk, rows_m // PIECE
        vmem, dma = pltpu.VMEM, pltpu.SemaphoreType.DMA
        whole = pl.BlockSpec(memory_space=pltpu.VMEM)
        turned, updated = pl.pallas_call(
            functools.partial(kernel, (n_k, n_s, n_z, n_y, chunk)),
            out_shape=(
                jax.ShapeDtypeStruct((width, rows_m), F32),
                jax.ShapeDtypeStruct((rows_h, cols), F32),
            ),
            in_specs=[pl.BlockSpec(memory_space=pl.ANY), whole, whole],
            out_specs=(whole, whole),
            scratch_shapes=[
                vmem((rows_m, cols), F32),
                vmem((rank, rows_m), F32),
                vmem((rows_m, rank), F32),
                vmem((rows_m, 3 * rank), BF16),
                vmem((rank, cols), F32),
                vmem((3 * rank, cols), BF16),
                vmem((3 * cols, rank), BF16),
                vmem((n_s, 8, rank), F32),
                vmem((8, rank), F32),
                vmem((rows_m, rank), F32),
                vmem((rows_m // 2, rank), F32),
                vmem((rows_m // 2, rank), F32),
                vmem((n_x - 1, rows_m // 2, rank), F32),
                vmem((rows_m, rank), F32),
                vmem((rank, rows_m), F32),
                vmem((rank, cols), F32),
                vmem((n_k, 8, rank), F32),
                vmem((8, rank), F32),
                vmem((n_y - 1, n_z, rows_h, cols), F32),
                vmem((n_z, rows_h, cols), F32),
                vmem((n_z - 1, rows_h, cols), F32),
                dma,
                dma((n_z,)),
                dma((n_z,)),
                dma((2 * n_z - 1, n_y - 1)),
                dma((n_k,)),
                dma((n_x - 1, pieces)),
                dma((pieces,)),
                dma((n_x - 1, pieces)),
                dma((n_s, pieces)),
                dma((n_s - 1,)),
                dma((n_s,)),
                dma((chunks,)),
                dma((chunks,)),
                dma((n_x - 1, chunks)),
                dma((n_x - 1, chunks)),
                dma((chunks,)),
                dma((chunks,)),
                dma((n_k - 1,)),
                dma((n_k,)),
                dma((n_y - 1, n_z, PARTS)),
                dma((n_y - 1, n_z, PARTS)),
                dma((n_z - 1, PARTS)),
                dma((n_z - 1, PARTS)),
            ],
            compiler_params=pltpu.CompilerParams(
                collective_id=0, has_side_effects=True, vmem_limit_bytes=56 * 2**20
            ),
            cost_estimate=pl.CostEstimate(
                flops=24 * rows_m * cols * rank,
                bytes_accessed=4 * rows_m * cols,
                transcendentals=2 * rows_m * cols,
            ),
        )(abundance, loadings.T, activity)
        return turned.T, updated

    in_specs = (P("kmer", "samp"), P("kmer", "samp"), P("kmer", "samp"))
    out_specs = (P("kmer", "samp"), P("kmer", "samp"))
    return jax.shard_map(
        per_device, mesh=mesh, in_specs=in_specs, out_specs=out_specs, check_vma=False
    )
```

```python
import functools

import jax
import jax.numpy as jnp
from jax import lax
from jax.experimental import pallas as pl
from jax.experimental.pallas import tpu as pltpu
from jax.sharding import PartitionSpec as P

F32, BF16 = jnp.float32, jnp.bfloat16
LANES = 128
PIECE = 512
PARTS = 2
FLYING = 3
CORES = 2


def halves(value):
    high = value.astype(BF16)
    return high, (value - high.astype(F32)).astype(BF16)


def quotient_of(above, below):
    guess = pl.reciprocal(below, approx=True)
    return above * (guess * (2.0 - below * guess))


def dot(a, b):
    return jnp.dot(a, b, preferred_element_type=F32)


def kernel(
    sizes, ab_hbm, load_ref, act_ref, newload_ref, newact_ref,
    ab, abt, wbuf, w3, hbuf, h3, ht3, tbuf, tsum, nbuf, recv_a, sbuf, recv_x, ubuf, acct, acc, cbuf, csum, column, recv_y, ybuf, recv_z,
    ab_sem, hr_s, hl_s, hy_s, h_r, wx_s, wc_s, wf_s, w_r, t_s, t_r, a_s, a_r, x_s, x_r, u_s, u_r, c_s, c_r,
    ry_s, ry_r, rz_s, rz_r,
):
    n_k, n_s, n_z, n_y, chunk = sizes
    n_x = n_s // CORES
    width, rows_m = load_ref.shape
    rows_h, cols = act_ref.shape
    rank = rows_h * n_k
    pieces = rows_m // PIECE
    chunks = rows_m // chunk
    half = rank // 2

    k, s = lax.axis_index("kmer"), lax.axis_index("samp")
    z, y = lax.div(k, n_y), lax.rem(k, n_y)
    x, core = lax.div(s, CORES), lax.rem(s, CORES)
    mate = x * CORES + (1 - core)

    def z_at(d):
        return lax.rem(z + d, n_z)

    def y_at(d):
        return lax.rem(y + d, n_y)

    def x_at(d):
        return lax.rem(x + d, n_x) * CORES + core

    def put(src, dst, send, recv, kk, ss):
        return pltpu.make_async_remote_copy(
            src_ref=src, dst_ref=dst, send_sem=send, recv_sem=recv,
            device_id={"kmer": kk, "samp": ss}, device_id_type=pl.DeviceIdType.MESH,
        )

    def block(start, size):
        return pl.ds(pl.multiple_of(start, size), size)

    def arrived(dst, sem):
        put(dst, dst, sem, sem, k, mate).wait_recv()

    sent = []

    def go(*args, when=None):
        copy = put(*args)
        sent.append((when, copy))
        if when is None:
            copy.start()
        else:
            pl.when(when)(copy.start)

    fetch = pltpu.make_async_copy(ab_hbm, ab, ab_sem)
    fetch.start()

    hbuf[block(k * rows_h, rows_h), :] = act_ref[...]
    wbuf[block(s * width, width), :] = load_ref[...]

    barrier = pltpu.get_barrier_semaphore()
    peers = [(lax.rem(k + d, n_k), s) for d in range(1, n_k)]
    peers += [(k, lax.rem(s + d, n_s)) for d in range(1, n_s)]
    for kk, ss in peers:
        pl.semaphore_signal(
            barrier, inc=1, device_id={"kmer": kk, "samp": ss}, device_id_type=pl.DeviceIdType.MESH
        )
    pl.semaphore_wait(barrier, len(peers))

    def hslot(kk):
        return hbuf.at[block(kk * rows_h, rows_h), :]

    def wslot(ss, j):
        return wbuf.at[block(ss * width, width), pl.ds(j * PIECE, PIECE)]

    def pass_h(zz, i, when):
        kk = zz * n_y + y
        slot = hslot(kk)
        up, down = jnp.minimum(z + 1, n_z - 1), jnp.maximum(z - 1, 0)
        if i >= 0:
            ok = z < n_z - 1
            go(slot, slot, hr_s.at[abs(i)], h_r.at[kk], up * n_y + y, s, when=ok if when is None else ok & when)
        if i <= 0:
            ok = z > 0
            go(slot, slot, hl_s.at[abs(i)], h_r.at[kk], down * n_y + y, s, when=ok if when is None else ok & when)
        for d in range(1, n_y):
            go(slot, slot, hy_s.at[n_z - 1 + i, d - 1], h_r.at[kk], z * n_y + y_at(d), s, when=when)

    pass_h(z, 0, None)
    for j in range(pieces):
        for d in range(1, n_x):
            go(wslot(s, j), wslot(s, j), wx_s.at[d - 1, j], w_r.at[s, j], k, x_at(d))
        go(wslot(s, j), wslot(s, j), wc_s.at[j], w_r.at[s, j], k, mate)

    def take_h(i):
        there = (z >= i) if i > 0 else (z - i <= n_z - 1)
        zz = jnp.clip(z - i, 0, n_z - 1)
        kk = zz * n_y + y

        @pl.when(there)
        def _():
            arrived(hslot(kk), h_r.at[kk])

        pass_h(zz, i, there)

    def take_w(j):
        for d in range(1, n_x):
            src = x_at(d)
            arrived(wslot(src, j), w_r.at[src, j])
            go(wslot(src, j), wslot(src, j), wf_s.at[d - 1, j], w_r.at[src, j], k, mate)

    waits = max(n_z - 1, pieces)
    turns = pl.cdiv(chunks, waits)
    for i in range(waits):
        if i < n_z - 1:
            take_h(i + 1)
            take_h(-i - 1)
        if i < pieces:
            take_w(i)
        if i == 0:
            fetch.wait()
        for at in range(i * turns * chunk, min((i + 1) * turns * chunk, rows_m), chunk):
            abt[:, at:at + chunk] = ab[at:at + chunk, :].T

    for j in range(pieces):
        for d in range(n_x):
            src = lax.rem(x + d, n_x) * CORES + (1 - core)
            arrived(wslot(src, j), w_r.at[src, j])
        at = slice(j * PIECE, (j + 1) * PIECE)
        high, low = halves(wbuf[:, at])
        w3[:, at] = jnp.concatenate([high, low, high], axis=0)

    for d in range(1, n_y):
        for i in range(n_z):
            src = i * n_y + y_at(d)
            arrived(hslot(src), h_r.at[src])

    high, low = halves(hbuf[...])
    h3[...] = jnp.concatenate([high, high, low], axis=1)
    turned = hbuf[...].T
    high, low = halves(turned)
    ht3[...] = jnp.concatenate([high, high, low], axis=1)
    tbuf[s] = jnp.broadcast_to(jnp.sum(turned, axis=0, keepdims=True), (8, rank))
    for d in range(1, n_s):
        go(tbuf.at[s], tbuf.at[s], t_s.at[d - 1], t_r.at[s], k, lax.rem(s + d, n_s))

    mine = block(core * half, half)

    def out_a(c):
        return put(
            nbuf.at[c, block((1 - core) * half, half), :], recv_a.at[c], a_s.at[c], a_r.at[c], k, mate
        )

    def out_x(c, d):
        return put(sbuf.at[c], recv_x.at[d - 1, c], x_s.at[d - 1, c], x_r.at[d - 1, c], k, x_at(d))

    def out_u(c):
        return put(ubuf.at[c, mine, :], ubuf.at[c, mine, :], u_s.at[c], u_r.at[c], k, mate)

    ahead = max(1, chunks // 2)

    def scale_rows(c):
        total = sbuf[c]
        for d in range(1, n_x):
            out_x(c, d).wait_recv()
            total = total + recv_x[d - 1, c]
        ubuf[c, mine, :] = wbuf[mine, block(c * chunk, chunk)] * total * tsum[mine, 0:1]
        out_u(c).start()

    def rows_step(c, carry):
        @pl.when(c < chunks)
        def _():
            rows = block(c * chunk, chunk)
            high, low = halves(quotient_of(abt[:, rows], dot(ht3[...], w3[:, rows])))
            nbuf[c] = dot(h3[...], jnp.concatenate([high, low, high], axis=0))
            out_a(c).start()

        @pl.when(c == 1)
        def _():
            for d in range(1, n_s):
                src = lax.rem(s + d, n_s)
                arrived(tbuf.at[src], t_r.at[src])
            totals = tbuf[0]
            for i in range(1, n_s):
                totals = totals + tbuf[i]
            tsum[...] = 1.0 / jnp.broadcast_to(totals[0:1, :], (LANES, rank)).T

        @pl.when(c != 1)
        def _():
            b = jnp.maximum(c - 1, 0)
            out_a(b).wait_recv()
            sbuf[b] = nbuf[b, mine, :] + recv_a[b]
            for d in range(1, n_x):
                out_x(b, d).start()

        @pl.when(c > ahead)
        def _():
            scale_rows(c - 1 - ahead)

        return carry

    lax.fori_loop(0, chunks + 1, rows_step, 0)
    acct[...] = jnp.zeros_like(acct)
    csum[...] = jnp.zeros_like(csum)

    def cols_step(c, carry):
        @pl.when((c < chunks) & (c >= chunks - ahead))
        def _():
            scale_rows(c)

        @pl.when(c >= 1)
        def _():
            b = c - 1
            out_u(b).wait_recv()
            updated = ubuf[b]
            high, low = halves(updated)
            rebuilt = dot(ht3[...], jnp.concatenate([high, low, high], axis=0))
            q_high, q_low = halves(quotient_of(abt[:, block(b * chunk, chunk)], rebuilt))
            turned = updated.T
            csum[...] += jnp.broadcast_to(jnp.sum(turned, axis=0, keepdims=True), csum.shape)
            high, low = halves(turned)
            acct[...] += dot(
                jnp.concatenate([q_high, q_high, q_low], axis=1), jnp.concatenate([high, low, high], axis=0)
            )

        return carry

    lax.fori_loop(0, chunks + 1, cols_step, 0)
    acc[...] = acct[...].T

    near = []
    for d in range(1, n_z // 2 + 1):
        near += [d] if d == n_z - d else [d, n_z - d]
    part = cols // PARTS
    steps = [(i, d, p) for i, d in enumerate(near[::-1] + [0]) for p in range(PARTS)]

    def part_of(p):
        return pl.ds(p * part, part)

    def send_y(i, d, p):
        for e in range(1, n_y):
            go(
                acc.at[block((z_at(d) * n_y + y_at(e)) * rows_h, rows_h), part_of(p)],
                recv_y.at[e - 1, i, :, part_of(p)],
                ry_s.at[e - 1, i, p], ry_r.at[e - 1, i, p], z * n_y + y_at(e), s,
            )

    for step in steps[:FLYING]:
        send_y(*step)
    cbuf[k] = csum[...]
    for d in range(1, n_k):
        go(cbuf.at[k], cbuf.at[k], c_s.at[d - 1], c_r.at[k], lax.rem(k + d, n_k), s)
    for c in range(chunks):
        newload_ref[:, c * chunk:(c + 1) * chunk] = ubuf[c, block(s * width, width), :]

    for at, (i, d, p) in enumerate(steps):
        for e in range(1, n_y):
            arrived(recv_y.at[e - 1, i, :, part_of(p)], ry_r.at[e - 1, i, p])
        if at + FLYING < len(steps):
            send_y(*steps[at + FLYING])
        total = acc[block((z_at(d) * n_y + y) * rows_h, rows_h), part_of(p)]
        for e in range(1, n_y):
            total = total + recv_y[e - 1, i, :, part_of(p)]
        ybuf[i, :, part_of(p)] = total
        if d:
            go(
                ybuf.at[i, :, part_of(p)], recv_z.at[i, :, part_of(p)],
                rz_s.at[i, p], rz_r.at[i, p], z_at(d) * n_y + y, s,
            )

    for d in range(1, n_k):
        src = lax.rem(k + d, n_k)
        arrived(cbuf.at[src], c_r.at[src])
    sums = cbuf[0, 0:1, :]
    for i in range(1, n_k):
        sums = sums + cbuf[i, 0:1, :]
    column[...] = jnp.broadcast_to(sums, (LANES, rank)).T
    scaled = act_ref[...] / column[block(k * rows_h, rows_h), 0:1]
    for p in range(PARTS):
        total = ybuf[n_z - 1, :, part_of(p)]
        for i in range(n_z - 1):
            arrived(recv_z.at[i, :, part_of(p)], rz_r.at[i, p])
            total = total + recv_z[i, :, part_of(p)]
        newact_ref[:, part_of(p)] = scaled[:, p * part:(p + 1) * part] * total

    for when, copy in sent:
        if when is None:
            copy.wait_send()
        else:
            pl.when(when)(copy.wait_send)

    def close(c, carry):
        out_a(c).wait_send()
        out_u(c).wait_send()
        for d in range(1, n_x):
            out_x(c, d).wait_send()
        return carry

    lax.fori_loop(0, chunks, close, 0)


def hand_over(load_in, act_in, load_out, act_out, sems):
    copies = [
        pltpu.make_async_copy(load_in, load_out, sems.at[0]),
        pltpu.make_async_copy(act_in, act_out, sems.at[1]),
    ]
    for copy in copies:
        copy.start()
    for copy in copies:
        copy.wait()


def solution(mesh):
    n_k, n_s = mesh.shape["kmer"], mesh.shape["samp"]
    n_y = max(d for d in range(1, n_k + 1) if n_k % d == 0 and d * d <= n_k)
    n_z, n_x = n_k // n_y, n_s // CORES

    def per_device(abundance, loadings, activity):
        rows_m, width = loadings.shape
        rows_h, cols = activity.shape
        rank = rows_h * n_k
        chunk = 256
        chunks, pieces = rows_m // chunk, rows_m // PIECE
        vmem, dma = pltpu.VMEM, pltpu.SemaphoreType.DMA
        whole = pl.BlockSpec(memory_space=pltpu.VMEM)
        turned, updated = pl.pallas_call(
            functools.partial(kernel, (n_k, n_s, n_z, n_y, chunk)),
            out_shape=(
                jax.ShapeDtypeStruct((width, rows_m), F32),
                jax.ShapeDtypeStruct((rows_h, cols), F32),
            ),
            in_specs=[pl.BlockSpec(memory_space=pl.ANY), whole, whole],
            out_specs=(whole, whole),
            scratch_shapes=[
                vmem((rows_m, cols), F32),
                vmem((cols, rows_m), F32),
                vmem((rank, rows_m), F32),
                vmem((3 * rank, rows_m), BF16),
                vmem((rank, cols), F32),
                vmem((rank, 3 * cols), BF16),
                vmem((cols, 3 * rank), BF16),
                vmem((n_s, 8, rank), F32),
                vmem((rank, LANES), F32),
                vmem((chunks, rank, chunk), F32),
                vmem((chunks, rank // 2, chunk), F32),
                vmem((chunks, rank // 2, chunk), F32),
                vmem((n_x - 1, chunks, rank // 2, chunk), F32),
                vmem((chunks, rank, chunk), F32),
                vmem((cols, rank), F32),
                vmem((rank, cols), F32),
                vmem((n_k, 8, rank), F32),
                vmem((8, rank), F32),
                vmem((rank, LANES), F32),
                vmem((n_y - 1, n_z, rows_h, cols), F32),
                vmem((n_z, rows_h, cols), F32),
                vmem((n_z - 1, rows_h, cols), F32),
                dma,
                dma((n_z,)),
                dma((n_z,)),
                dma((2 * n_z - 1, n_y - 1)),
                dma((n_k,)),
                dma((n_x - 1, pieces)),
                dma((pieces,)),
                dma((n_x - 1, pieces)),
                dma((n_s, pieces)),
                dma((n_s - 1,)),
                dma((n_s,)),
                dma((chunks,)),
                dma((chunks,)),
                dma((n_x - 1, chunks)),
                dma((n_x - 1, chunks)),
                dma((chunks,)),
                dma((chunks,)),
                dma((n_k - 1,)),
                dma((n_k,)),
                dma((n_y - 1, n_z, PARTS)),
                dma((n_y - 1, n_z, PARTS)),
                dma((n_z - 1, PARTS)),
                dma((n_z - 1, PARTS)),
            ],
            compiler_params=pltpu.CompilerParams(
                collective_id=0, has_side_effects=True, vmem_limit_bytes=56 * 2**20
            ),
            cost_estimate=pl.CostEstimate(
                flops=24 * rows_m * cols * rank,
                bytes_accessed=4 * rows_m * cols,
                transcendentals=2 * rows_m * cols,
            ),
        )(abundance, loadings.T, activity)
        anywhere = pl.BlockSpec(memory_space=pl.ANY)
        turned, updated = pl.pallas_call(
            hand_over,
            out_shape=(
                jax.ShapeDtypeStruct((width, rows_m), F32),
                jax.ShapeDtypeStruct((rows_h, cols), F32),
            ),
            in_specs=[anywhere, anywhere],
            out_specs=(anywhere, anywhere),
            scratch_shapes=[dma((2,))],
            compiler_params=pltpu.CompilerParams(vmem_limit_bytes=56 * 2**20),
        )(turned, updated)
        return turned.T, updated

    in_specs = (P("kmer", "samp"), P("kmer", "samp"), P("kmer", "samp"))
    out_specs = (P("kmer", "samp"), P("kmer", "samp"))
    return jax.shard_map(
        per_device, mesh=mesh, in_specs=in_specs, out_specs=out_specs, check_vma=False
    )
```

```python
import functools

import jax
import jax.numpy as jnp
from jax import lax
from jax.experimental import pallas as pl
from jax.experimental.pallas import tpu as pltpu
from jax.sharding import PartitionSpec as P

F32, BF16 = jnp.float32, jnp.bfloat16
LANES = 128
PIECE = 512
PARTS = 2
FLYING = 3
HOPS = 2
CORES = 2


def halves(value):
    high = value.astype(BF16)
    return high, (value - high.astype(F32)).astype(BF16)


def quotient_of(above, below):
    guess = pl.reciprocal(below, approx=True)
    return above * (guess * (2.0 - below * guess))


def dot(a, b):
    return jnp.dot(a, b, preferred_element_type=F32)


def kernel(
    sizes, ab_hbm, load_ref, act_ref, newload_ref, newact_ref,
    ab, abt, wbuf, w3, hbuf, h3, ht3, tbuf, tsum, nbuf, recv_a, sbuf, recv_x, ubuf, acct, acc, cbuf, csum, column, recv_y, ybuf, recv_z,
    ab_sem, hr_s, hl_s, hy_s, h_r, wx_s, wc_s, wf_s, w_r, t_s, t_r, a_s, a_r, x_s, x_r, u_s, u_r, c_s, c_r,
    ry_s, ry_r, rz_s, rz_r,
):
    n_k, n_s, n_z, n_y, chunk = sizes
    n_x = n_s // CORES
    width, rows_m = load_ref.shape
    rows_h, cols = act_ref.shape
    rank = rows_h * n_k
    pieces = rows_m // PIECE
    chunks = rows_m // chunk
    half = rank // 2

    k, s = lax.axis_index("kmer"), lax.axis_index("samp")
    z, y = lax.div(k, n_y), lax.rem(k, n_y)
    x, core = lax.div(s, CORES), lax.rem(s, CORES)
    mate = x * CORES + (1 - core)

    def z_at(d):
        return lax.rem(z + d, n_z)

    def y_at(d):
        return lax.rem(y + d, n_y)

    def x_at(d):
        return lax.rem(x + d, n_x) * CORES + core

    def put(src, dst, send, recv, kk, ss):
        return pltpu.make_async_remote_copy(
            src_ref=src, dst_ref=dst, send_sem=send, recv_sem=recv,
            device_id={"kmer": kk, "samp": ss}, device_id_type=pl.DeviceIdType.MESH,
        )

    def block(start, size):
        return pl.ds(pl.multiple_of(start, size), size)

    def arrived(dst, sem):
        put(dst, dst, sem, sem, k, mate).wait_recv()

    sent = []

    def go(*args, when=None):
        copy = put(*args)
        sent.append((when, copy))
        if when is None:
            copy.start()
        else:
            pl.when(when)(copy.start)

    def fetch(c):
        rows = pl.ds(c * chunk, chunk)
        return pltpu.make_async_copy(ab_hbm.at[rows, :], ab.at[rows, :], ab_sem.at[c])

    for c in range(chunks):
        fetch(c).start()

    hbuf[block(k * rows_h, rows_h), :] = act_ref[...]
    wbuf[block(s * width, width), :] = load_ref[...]

    barrier = pltpu.get_barrier_semaphore()
    peers = [(lax.rem(k + d, n_k), s) for d in range(1, n_k)]
    peers += [(k, lax.rem(s + d, n_s)) for d in range(1, n_s)]
    for kk, ss in peers:
        pl.semaphore_signal(
            barrier, inc=1, device_id={"kmer": kk, "samp": ss}, device_id_type=pl.DeviceIdType.MESH
        )
    pl.semaphore_wait(barrier, len(peers))

    part_h = cols // HOPS

    def hslot(kk, p):
        return hbuf.at[block(kk * rows_h, rows_h), pl.ds(p * part_h, part_h)]

    def wslot(ss, j):
        return wbuf.at[block(ss * width, width), pl.ds(j * PIECE, PIECE)]

    def pass_h(zz, i, p, when):
        kk = zz * n_y + y
        slot, recv = hslot(kk, p), h_r.at[kk, p]
        up, down = jnp.minimum(z + 1, n_z - 1), jnp.maximum(z - 1, 0)
        if i >= 0:
            ok = z < n_z - 1
            go(slot, slot, hr_s.at[abs(i), p], recv, up * n_y + y, s, when=ok if when is None else ok & when)
        if i <= 0:
            ok = z > 0
            go(slot, slot, hl_s.at[abs(i), p], recv, down * n_y + y, s, when=ok if when is None else ok & when)
        for d in range(1, n_y):
            go(slot, slot, hy_s.at[n_z - 1 + i, d - 1, p], recv, z * n_y + y_at(d), s, when=when)

    for p in range(HOPS):
        pass_h(z, 0, p, None)
    for j in range(pieces):
        for d in range(1, n_x):
            go(wslot(s, j), wslot(s, j), wx_s.at[d - 1, j], w_r.at[s, j], k, x_at(d))
        go(wslot(s, j), wslot(s, j), wc_s.at[j], w_r.at[s, j], k, mate)

    def take_h(i, p):
        there = (z >= i) if i > 0 else (z - i <= n_z - 1)
        zz = jnp.clip(z - i, 0, n_z - 1)
        kk = zz * n_y + y

        @pl.when(there)
        def _():
            arrived(hslot(kk, p), h_r.at[kk, p])

        pass_h(zz, i, p, there)

    def take_w(j):
        for d in range(1, n_x):
            src = x_at(d)
            arrived(wslot(src, j), w_r.at[src, j])
            go(wslot(src, j), wslot(src, j), wf_s.at[d - 1, j], w_r.at[src, j], k, mate)

    waits = max(n_z - 1, pieces)
    turns = pl.cdiv(chunks, waits)
    for i in range(waits):
        if i < n_z - 1:
            for p in range(HOPS):
                take_h(i + 1, p)
                take_h(-i - 1, p)
        if i < pieces:
            take_w(i)
        for c in range(i * turns, min((i + 1) * turns, chunks)):
            fetch(c).wait()
            at = slice(c * chunk, (c + 1) * chunk)
            abt[:, at] = ab[at, :].T

    for j in range(pieces):
        for d in range(n_x):
            src = lax.rem(x + d, n_x) * CORES + (1 - core)
            arrived(wslot(src, j), w_r.at[src, j])
        at = slice(j * PIECE, (j + 1) * PIECE)
        high, low = halves(wbuf[:, at])
        w3[:, at] = jnp.concatenate([high, low, high], axis=0)

    row_totals = jnp.zeros((1, rank), F32)
    for p in range(HOPS):
        for d in range(1, n_y):
            for i in range(n_z):
                src = i * n_y + y_at(d)
                arrived(hslot(src, p), h_r.at[src, p])
        at = slice(p * part_h, (p + 1) * part_h)
        high, low = halves(hbuf[:, at])
        h3[:, at], h3[:, cols + p * part_h:cols + (p + 1) * part_h] = high, high
        h3[:, 2 * cols + p * part_h:2 * cols + (p + 1) * part_h] = low
        turned = hbuf[:, at].T
        high, low = halves(turned)
        ht3[at, :] = jnp.concatenate([high, high, low], axis=1)
        row_totals = row_totals + jnp.sum(turned, axis=0, keepdims=True)
    tbuf[s] = jnp.broadcast_to(row_totals, (8, rank))
    for d in range(1, n_s):
        go(tbuf.at[s], tbuf.at[s], t_s.at[d - 1], t_r.at[s], k, lax.rem(s + d, n_s))

    mine = block(core * half, half)

    def out_a(c):
        return put(
            nbuf.at[c, block((1 - core) * half, half), :], recv_a.at[c], a_s.at[c], a_r.at[c], k, mate
        )

    def out_x(c, d):
        return put(sbuf.at[c], recv_x.at[d - 1, c], x_s.at[d - 1, c], x_r.at[d - 1, c], k, x_at(d))

    def out_u(c):
        return put(ubuf.at[c, mine, :], ubuf.at[c, mine, :], u_s.at[c], u_r.at[c], k, mate)

    ahead = max(1, chunks // 2)

    def scale_rows(c):
        total = sbuf[c]
        for d in range(1, n_x):
            out_x(c, d).wait_recv()
            total = total + recv_x[d - 1, c]
        ubuf[c, mine, :] = wbuf[mine, block(c * chunk, chunk)] * total * tsum[mine, 0:1]
        out_u(c).start()

    def rows_step(c, carry):
        @pl.when(c < chunks)
        def _():
            rows = block(c * chunk, chunk)
            high, low = halves(quotient_of(abt[:, rows], dot(ht3[...], w3[:, rows])))
            nbuf[c] = dot(h3[...], jnp.concatenate([high, low, high], axis=0))
            out_a(c).start()

        @pl.when(c == 1)
        def _():
            for d in range(1, n_s):
                src = lax.rem(s + d, n_s)
                arrived(tbuf.at[src], t_r.at[src])
            totals = tbuf[0]
            for i in range(1, n_s):
                totals = totals + tbuf[i]
            tsum[...] = 1.0 / jnp.broadcast_to(totals[0:1, :], (LANES, rank)).T

        @pl.when(c != 1)
        def _():
            b = jnp.maximum(c - 1, 0)
            out_a(b).wait_recv()
            sbuf[b] = nbuf[b, mine, :] + recv_a[b]
            for d in range(1, n_x):
                out_x(b, d).start()

        @pl.when(c > ahead)
        def _():
            scale_rows(c - 1 - ahead)

        return carry

    lax.fori_loop(0, chunks + 1, rows_step, 0)
    acct[...] = jnp.zeros_like(acct)
    csum[...] = jnp.zeros_like(csum)

    def cols_step(c, carry):
        @pl.when((c < chunks) & (c >= chunks - ahead))
        def _():
            scale_rows(c)

        @pl.when(c >= 1)
        def _():
            b = c - 1
            out_u(b).wait_recv()
            updated = ubuf[b]
            high, low = halves(updated)
            rebuilt = dot(ht3[...], jnp.concatenate([high, low, high], axis=0))
            q_high, q_low = halves(quotient_of(abt[:, block(b * chunk, chunk)], rebuilt))
            turned = updated.T
            csum[...] += jnp.broadcast_to(jnp.sum(turned, axis=0, keepdims=True), csum.shape)
            high, low = halves(turned)
            acct[...] += dot(
                jnp.concatenate([q_high, q_high, q_low], axis=1), jnp.concatenate([high, low, high], axis=0)
            )

        return carry

    lax.fori_loop(0, chunks + 1, cols_step, 0)
    acc[...] = acct[...].T

    near = []
    for d in range(1, n_z // 2 + 1):
        near += [d] if d == n_z - d else [d, n_z - d]
    part = cols // PARTS
    steps = [(i, d, p) for i, d in enumerate(near[::-1] + [0]) for p in range(PARTS)]

    def part_of(p):
        return pl.ds(p * part, part)

    def send_y(i, d, p):
        for e in range(1, n_y):
            go(
                acc.at[block((z_at(d) * n_y + y_at(e)) * rows_h, rows_h), part_of(p)],
                recv_y.at[e - 1, i, :, part_of(p)],
                ry_s.at[e - 1, i, p], ry_r.at[e - 1, i, p], z * n_y + y_at(e), s,
            )

    for step in steps[:FLYING]:
        send_y(*step)
    cbuf[k] = csum[...]
    for d in range(1, n_k):
        go(cbuf.at[k], cbuf.at[k], c_s.at[d - 1], c_r.at[k], lax.rem(k + d, n_k), s)
    for c in range(chunks):
        newload_ref[:, c * chunk:(c + 1) * chunk] = ubuf[c, block(s * width, width), :]

    for at, (i, d, p) in enumerate(steps):
        for e in range(1, n_y):
            arrived(recv_y.at[e - 1, i, :, part_of(p)], ry_r.at[e - 1, i, p])
        if at + FLYING < len(steps):
            send_y(*steps[at + FLYING])
        total = acc[block((z_at(d) * n_y + y) * rows_h, rows_h), part_of(p)]
        for e in range(1, n_y):
            total = total + recv_y[e - 1, i, :, part_of(p)]
        ybuf[i, :, part_of(p)] = total
        if d:
            go(
                ybuf.at[i, :, part_of(p)], recv_z.at[i, :, part_of(p)],
                rz_s.at[i, p], rz_r.at[i, p], z_at(d) * n_y + y, s,
            )

    for d in range(1, n_k):
        src = lax.rem(k + d, n_k)
        arrived(cbuf.at[src], c_r.at[src])
    sums = cbuf[0, 0:1, :]
    for i in range(1, n_k):
        sums = sums + cbuf[i, 0:1, :]
    column[...] = jnp.broadcast_to(sums, (LANES, rank)).T
    scaled = act_ref[...] / column[block(k * rows_h, rows_h), 0:1]
    for p in range(PARTS):
        total = ybuf[n_z - 1, :, part_of(p)]
        for i in range(n_z - 1):
            arrived(recv_z.at[i, :, part_of(p)], rz_r.at[i, p])
            total = total + recv_z[i, :, part_of(p)]
        newact_ref[:, part_of(p)] = scaled[:, p * part:(p + 1) * part] * total

    for when, copy in sent:
        if when is None:
            copy.wait_send()
        else:
            pl.when(when)(copy.wait_send)

    def close(c, carry):
        out_a(c).wait_send()
        out_u(c).wait_send()
        for d in range(1, n_x):
            out_x(c, d).wait_send()
        return carry

    lax.fori_loop(0, chunks, close, 0)


def hand_over(load_in, act_in, load_out, act_out):
    load_out[...] = load_in[...]
    act_out[...] = act_in[...]


def solution(mesh):
    n_k, n_s = mesh.shape["kmer"], mesh.shape["samp"]
    n_y = max(d for d in range(1, n_k + 1) if n_k % d == 0 and d * d <= n_k)
    n_z, n_x = n_k // n_y, n_s // CORES

    def per_device(abundance, loadings, activity):
        rows_m, width = loadings.shape
        rows_h, cols = activity.shape
        rank = rows_h * n_k
        chunk = 256
        chunks, pieces = rows_m // chunk, rows_m // PIECE
        vmem, dma = pltpu.VMEM, pltpu.SemaphoreType.DMA
        whole = pl.BlockSpec(memory_space=pltpu.VMEM)
        turned, updated = pl.pallas_call(
            functools.partial(kernel, (n_k, n_s, n_z, n_y, chunk)),
            out_shape=(
                jax.ShapeDtypeStruct((width, rows_m), F32),
                jax.ShapeDtypeStruct((rows_h, cols), F32),
            ),
            in_specs=[pl.BlockSpec(memory_space=pl.ANY), whole, whole],
            out_specs=(whole, whole),
            scratch_shapes=[
                vmem((rows_m, cols), F32),
                vmem((cols, rows_m), F32),
                vmem((rank, rows_m), F32),
                vmem((3 * rank, rows_m), BF16),
                vmem((rank, cols), F32),
                vmem((rank, 3 * cols), BF16),
                vmem((cols, 3 * rank), BF16),
                vmem((n_s, 8, rank), F32),
                vmem((rank, LANES), F32),
                vmem((chunks, rank, chunk), F32),
                vmem((chunks, rank // 2, chunk), F32),
                vmem((chunks, rank // 2, chunk), F32),
                vmem((n_x - 1, chunks, rank // 2, chunk), F32),
                vmem((chunks, rank, chunk), F32),
                vmem((cols, rank), F32),
                vmem((rank, cols), F32),
                vmem((n_k, 8, rank), F32),
                vmem((8, rank), F32),
                vmem((rank, LANES), F32),
                vmem((n_y - 1, n_z, rows_h, cols), F32),
                vmem((n_z, rows_h, cols), F32),
                vmem((n_z - 1, rows_h, cols), F32),
                dma((chunks,)),
                dma((n_z, HOPS)),
                dma((n_z, HOPS)),
                dma((2 * n_z - 1, n_y - 1, HOPS)),
                dma((n_k, HOPS)),
                dma((n_x - 1, pieces)),
                dma((pieces,)),
                dma((n_x - 1, pieces)),
                dma((n_s, pieces)),
                dma((n_s - 1,)),
                dma((n_s,)),
                dma((chunks,)),
                dma((chunks,)),
                dma((n_x - 1, chunks)),
                dma((n_x - 1, chunks)),
                dma((chunks,)),
                dma((chunks,)),
                dma((n_k - 1,)),
                dma((n_k,)),
                dma((n_y - 1, n_z, PARTS)),
                dma((n_y - 1, n_z, PARTS)),
                dma((n_z - 1, PARTS)),
                dma((n_z - 1, PARTS)),
            ],
            compiler_params=pltpu.CompilerParams(
                collective_id=0, has_side_effects=True, vmem_limit_bytes=56 * 2**20
            ),
            cost_estimate=pl.CostEstimate(
                flops=24 * rows_m * cols * rank,
                bytes_accessed=4 * rows_m * cols,
                transcendentals=2 * rows_m * cols,
            ),
        )(abundance, loadings.T, activity)
        turned, updated = pl.pallas_call(
            hand_over,
            out_shape=(
                jax.ShapeDtypeStruct((width, rows_m), F32),
                jax.ShapeDtypeStruct((rows_h, cols), F32),
            ),
            in_specs=[whole, whole],
            out_specs=(whole, whole),
        )(turned, updated)
        return turned.T, updated

    in_specs = (P("kmer", "samp"), P("kmer", "samp"), P("kmer", "samp"))
    out_specs = (P("kmer", "samp"), P("kmer", "samp"))
    return jax.shard_map(
        per_device, mesh=mesh, in_specs=in_specs, out_specs=out_specs, check_vma=False
    )
```

```python
import functools

import jax
import jax.numpy as jnp
from jax import lax
from jax.experimental import pallas as pl
from jax.experimental.pallas import tpu as pltpu
from jax.sharding import PartitionSpec as P

F32, BF16 = jnp.float32, jnp.bfloat16
LANES = 128
PIECE = 512
PARTS = 2
FLYING = 3
HOPS = 2
CORES = 2


def halves(value):
    high = value.astype(BF16)
    return high, (value - high.astype(F32)).astype(BF16)


def quotient_of(above, below):
    guess = pl.reciprocal(below, approx=True)
    return above * (guess * (2.0 - below * guess))


def dot(a, b):
    return jnp.dot(a, b, preferred_element_type=F32)


def kernel(
    sizes, ab_hbm, load_ref, act_ref, newload_ref, newact_ref,
    ab, abt, wbuf, w3, hbuf, h3, ht3, tbuf, tsum, nbuf, recv_a, sbuf, recv_x, ubuf, acct, acc, cbuf, csum, column, recv_y, ybuf, recv_z,
    ab_sem, hr_s, hl_s, hy_s, h_r, wx_s, wc_s, wf_s, w_r, t_s, t_r, a_s, a_r, x_s, x_r, u_s, u_r, c_s, c_r,
    ry_s, ry_r, rz_s, rz_r,
):
    n_k, n_s, n_z, n_y, chunk = sizes
    n_x = n_s // CORES
    width, rows_m = load_ref.shape
    rows_h, cols = act_ref.shape
    rank = rows_h * n_k
    pieces = rows_m // PIECE
    chunks = rows_m // chunk
    half = rank // 2

    k, s = lax.axis_index("kmer"), lax.axis_index("samp")
    z, y = lax.div(k, n_y), lax.rem(k, n_y)
    x, core = lax.div(s, CORES), lax.rem(s, CORES)
    mate = x * CORES + (1 - core)

    def z_at(d):
        return lax.rem(z + d, n_z)

    def y_at(d):
        return lax.rem(y + d, n_y)

    def x_at(d):
        return lax.rem(x + d, n_x) * CORES + core

    def put(src, dst, send, recv, kk, ss):
        return pltpu.make_async_remote_copy(
            src_ref=src, dst_ref=dst, send_sem=send, recv_sem=recv,
            device_id={"kmer": kk, "samp": ss}, device_id_type=pl.DeviceIdType.MESH,
        )

    def block(start, size):
        return pl.ds(pl.multiple_of(start, size), size)

    def arrived(dst, sem):
        put(dst, dst, sem, sem, k, mate).wait_recv()

    sent = []

    def go(*args, when=None):
        copy = put(*args)
        sent.append((when, copy))
        if when is None:
            copy.start()
        else:
            pl.when(when)(copy.start)

    def fetch(c):
        rows = pl.ds(c * chunk, chunk)
        return pltpu.make_async_copy(ab_hbm.at[rows, :], ab.at[rows, :], ab_sem.at[c])

    for c in range(chunks):
        fetch(c).start()

    hbuf[block(k * rows_h, rows_h), :] = act_ref[...]
    wbuf[block(s * width, width), :] = load_ref[...]

    barrier = pltpu.get_barrier_semaphore()
    peers = [(lax.rem(k + d, n_k), s) for d in range(1, n_k)]
    peers += [(k, lax.rem(s + d, n_s)) for d in range(1, n_s)]
    for kk, ss in peers:
        pl.semaphore_signal(
            barrier, inc=1, device_id={"kmer": kk, "samp": ss}, device_id_type=pl.DeviceIdType.MESH
        )
    pl.semaphore_wait(barrier, len(peers))

    part_h = cols // HOPS

    def hslot(kk, p):
        return hbuf.at[block(kk * rows_h, rows_h), pl.ds(p * part_h, part_h)]

    def wslot(ss, j):
        return wbuf.at[block(ss * width, width), pl.ds(j * PIECE, PIECE)]

    def pass_h(zz, i, p, when):
        kk = zz * n_y + y
        slot, recv = hslot(kk, p), h_r.at[kk, p]
        up, down = jnp.minimum(z + 1, n_z - 1), jnp.maximum(z - 1, 0)
        if i >= 0:
            ok = z < n_z - 1
            go(slot, slot, hr_s.at[abs(i), p], recv, up * n_y + y, s, when=ok if when is None else ok & when)
        if i <= 0:
            ok = z > 0
            go(slot, slot, hl_s.at[abs(i), p], recv, down * n_y + y, s, when=ok if when is None else ok & when)
        for d in range(1, n_y):
            go(slot, slot, hy_s.at[n_z - 1 + i, d - 1, p], recv, z * n_y + y_at(d), s, when=when)

    for p in range(HOPS):
        pass_h(z, 0, p, None)
    for j in range(pieces):
        for d in range(1, n_x):
            go(wslot(s, j), wslot(s, j), wx_s.at[d - 1, j], w_r.at[s, j], k, x_at(d))
        go(wslot(s, j), wslot(s, j), wc_s.at[j], w_r.at[s, j], k, mate)

    def take_h(i, p):
        there = (z >= i) if i > 0 else (z - i <= n_z - 1)
        zz = jnp.clip(z - i, 0, n_z - 1)
        kk = zz * n_y + y

        @pl.when(there)
        def _():
            arrived(hslot(kk, p), h_r.at[kk, p])

        pass_h(zz, i, p, there)

    def take_w(j):
        for d in range(1, n_x):
            src = x_at(d)
            arrived(wslot(src, j), w_r.at[src, j])
            go(wslot(src, j), wslot(src, j), wf_s.at[d - 1, j], w_r.at[src, j], k, mate)

    waits = max(n_z - 1, pieces)
    turns = pl.cdiv(chunks, waits)
    for i in range(waits):
        if i < n_z - 1:
            for p in range(HOPS):
                take_h(i + 1, p)
                take_h(-i - 1, p)
        if i < pieces:
            take_w(i)
        for c in range(i * turns, min((i + 1) * turns, chunks)):
            fetch(c).wait()
            at = slice(c * chunk, (c + 1) * chunk)
            abt[:, at] = ab[at, :].T

    for j in range(pieces):
        for d in range(n_x):
            src = lax.rem(x + d, n_x) * CORES + (1 - core)
            arrived(wslot(src, j), w_r.at[src, j])
        at = slice(j * PIECE, (j + 1) * PIECE)
        high, low = halves(wbuf[:, at])
        w3[:, at] = jnp.concatenate([high, low, high], axis=0)

    row_totals = jnp.zeros((1, rank), F32)
    for p in range(HOPS):
        for d in range(1, n_y):
            for i in range(n_z):
                src = i * n_y + y_at(d)
                arrived(hslot(src, p), h_r.at[src, p])
        at = slice(p * part_h, (p + 1) * part_h)
        high, low = halves(hbuf[:, at])
        h3[:, at], h3[:, cols + p * part_h:cols + (p + 1) * part_h] = high, high
        h3[:, 2 * cols + p * part_h:2 * cols + (p + 1) * part_h] = low
        turned = hbuf[:, at].T
        high, low = halves(turned)
        ht3[at, :] = jnp.concatenate([high, high, low], axis=1)
        row_totals = row_totals + jnp.sum(turned, axis=0, keepdims=True)
    tbuf[s] = jnp.broadcast_to(row_totals, (8, rank))
    for d in range(1, n_s):
        go(tbuf.at[s], tbuf.at[s], t_s.at[d - 1], t_r.at[s], k, lax.rem(s + d, n_s))

    mine = block(core * half, half)

    def out_a(c):
        return put(
            nbuf.at[c, block((1 - core) * half, half), :], recv_a.at[c], a_s.at[c], a_r.at[c], k, mate
        )

    def out_x(c, d):
        return put(sbuf.at[c], recv_x.at[d - 1, c], x_s.at[d - 1, c], x_r.at[d - 1, c], k, x_at(d))

    def out_u(c):
        return put(ubuf.at[c, mine, :], ubuf.at[c, mine, :], u_s.at[c], u_r.at[c], k, mate)

    ahead = max(1, chunks // 2)

    def scale_rows(c):
        total = sbuf[c]
        for d in range(1, n_x):
            out_x(c, d).wait_recv()
            total = total + recv_x[d - 1, c]
        ubuf[c, mine, :] = wbuf[mine, block(c * chunk, chunk)] * total * tsum[mine, 0:1]
        out_u(c).start()

    def rows_step(c, carry):
        @pl.when(c < chunks)
        def _():
            rows = block(c * chunk, chunk)
            high, low = halves(quotient_of(abt[:, rows], dot(ht3[...], w3[:, rows])))
            nbuf[c] = dot(h3[...], jnp.concatenate([high, low, high], axis=0))
            out_a(c).start()

        @pl.when(c == 1)
        def _():
            for d in range(1, n_s):
                src = lax.rem(s + d, n_s)
                arrived(tbuf.at[src], t_r.at[src])
            totals = tbuf[0]
            for i in range(1, n_s):
                totals = totals + tbuf[i]
            tsum[...] = 1.0 / jnp.broadcast_to(totals[0:1, :], (LANES, rank)).T

        @pl.when(c != 1)
        def _():
            b = jnp.maximum(c - 1, 0)
            out_a(b).wait_recv()
            sbuf[b] = nbuf[b, mine, :] + recv_a[b]
            for d in range(1, n_x):
                out_x(b, d).start()

        @pl.when(c > ahead)
        def _():
            scale_rows(c - 1 - ahead)

        return carry

    lax.fori_loop(0, chunks + 1, rows_step, 0)
    acct[...] = jnp.zeros_like(acct)
    csum[...] = jnp.zeros_like(csum)

    def cols_step(c, carry):
        @pl.when((c < chunks) & (c >= chunks - ahead))
        def _():
            scale_rows(c)

        @pl.when(c >= 1)
        def _():
            b = c - 1
            out_u(b).wait_recv()
            updated = ubuf[b]
            high, low = halves(updated)
            rebuilt = dot(ht3[...], jnp.concatenate([high, low, high], axis=0))
            q_high, q_low = halves(quotient_of(abt[:, block(b * chunk, chunk)], rebuilt))
            turned = updated.T
            csum[...] += jnp.broadcast_to(jnp.sum(turned, axis=0, keepdims=True), csum.shape)
            high, low = halves(turned)
            acct[...] += dot(
                jnp.concatenate([q_high, q_high, q_low], axis=1), jnp.concatenate([high, low, high], axis=0)
            )

        return carry

    lax.fori_loop(0, chunks + 1, cols_step, 0)
    acc[...] = acct[...].T

    near = []
    for d in range(1, n_z // 2 + 1):
        near += [d] if d == n_z - d else [d, n_z - d]
    part = cols // PARTS
    steps = [(i, d, p) for i, d in enumerate(near[::-1] + [0]) for p in range(PARTS)]

    def part_of(p):
        return pl.ds(p * part, part)

    def send_y(i, d, p):
        for e in range(1, n_y):
            go(
                acc.at[block((z_at(d) * n_y + y_at(e)) * rows_h, rows_h), part_of(p)],
                recv_y.at[e - 1, i, :, part_of(p)],
                ry_s.at[e - 1, i, p], ry_r.at[e - 1, i, p], z * n_y + y_at(e), s,
            )

    for step in steps[:FLYING]:
        send_y(*step)
    cbuf[k] = csum[...]
    for d in range(1, n_k):
        go(cbuf.at[k], cbuf.at[k], c_s.at[d - 1], c_r.at[k], lax.rem(k + d, n_k), s)
    for c in range(chunks):
        newload_ref[:, c * chunk:(c + 1) * chunk] = ubuf[c, block(s * width, width), :]

    for at, (i, d, p) in enumerate(steps):
        for e in range(1, n_y):
            arrived(recv_y.at[e - 1, i, :, part_of(p)], ry_r.at[e - 1, i, p])
        if at + FLYING < len(steps):
            send_y(*steps[at + FLYING])
        total = acc[block((z_at(d) * n_y + y) * rows_h, rows_h), part_of(p)]
        for e in range(1, n_y):
            total = total + recv_y[e - 1, i, :, part_of(p)]
        ybuf[i, :, part_of(p)] = total
        if d:
            go(
                ybuf.at[i, :, part_of(p)], recv_z.at[i, :, part_of(p)],
                rz_s.at[i, p], rz_r.at[i, p], z_at(d) * n_y + y, s,
            )

    for d in range(1, n_k):
        src = lax.rem(k + d, n_k)
        arrived(cbuf.at[src], c_r.at[src])
    sums = cbuf[0, 0:1, :]
    for i in range(1, n_k):
        sums = sums + cbuf[i, 0:1, :]
    column[...] = jnp.broadcast_to(sums, (LANES, rank)).T
    scaled = act_ref[...] / column[block(k * rows_h, rows_h), 0:1]
    for p in range(PARTS):
        total = ybuf[n_z - 1, :, part_of(p)]
        for i in range(n_z - 1):
            arrived(recv_z.at[i, :, part_of(p)], rz_r.at[i, p])
            total = total + recv_z[i, :, part_of(p)]
        newact_ref[:, part_of(p)] = scaled[:, p * part:(p + 1) * part] * total

    for when, copy in sent:
        if when is None:
            copy.wait_send()
        else:
            pl.when(when)(copy.wait_send)

    def close(c, carry):
        out_a(c).wait_send()
        out_u(c).wait_send()
        for d in range(1, n_x):
            out_x(c, d).wait_send()
        return carry

    lax.fori_loop(0, chunks, close, 0)


def hand_over(load_in, act_in, load_out, act_out):
    load_out[...] = load_in[...]
    act_out[...] = act_in[...]


def solution(mesh):
    n_k, n_s = mesh.shape["kmer"], mesh.shape["samp"]
    n_y = max(d for d in range(1, n_k + 1) if n_k % d == 0 and d * d <= n_k)
    n_z, n_x = n_k // n_y, n_s // CORES

    def per_device(abundance, loadings, activity):
        rows_m, width = loadings.shape
        rows_h, cols = activity.shape
        rank = rows_h * n_k
        chunk = 512
        chunks, pieces = rows_m // chunk, rows_m // PIECE
        vmem, dma = pltpu.VMEM, pltpu.SemaphoreType.DMA
        whole = pl.BlockSpec(memory_space=pltpu.VMEM)
        turned, updated = pl.pallas_call(
            functools.partial(kernel, (n_k, n_s, n_z, n_y, chunk)),
            out_shape=(
                jax.ShapeDtypeStruct((width, rows_m), F32),
                jax.ShapeDtypeStruct((rows_h, cols), F32),
            ),
            in_specs=[pl.BlockSpec(memory_space=pl.ANY), whole, whole],
            out_specs=(whole, whole),
            scratch_shapes=[
                vmem((rows_m, cols), F32),
                vmem((cols, rows_m), F32),
                vmem((rank, rows_m), F32),
                vmem((3 * rank, rows_m), BF16),
                vmem((rank, cols), F32),
                vmem((rank, 3 * cols), BF16),
                vmem((cols, 3 * rank), BF16),
                vmem((n_s, 8, rank), F32),
                vmem((rank, LANES), F32),
                vmem((chunks, rank, chunk), F32),
                vmem((chunks, rank // 2, chunk), F32),
                vmem((chunks, rank // 2, chunk), F32),
                vmem((n_x - 1, chunks, rank // 2, chunk), F32),
                vmem((chunks, rank, chunk), F32),
                vmem((cols, rank), F32),
                vmem((rank, cols), F32),
                vmem((n_k, 8, rank), F32),
                vmem((8, rank), F32),
                vmem((rank, LANES), F32),
                vmem((n_y - 1, n_z, rows_h, cols), F32),
                vmem((n_z, rows_h, cols), F32),
                vmem((n_z - 1, rows_h, cols), F32),
                dma((chunks,)),
                dma((n_z, HOPS)),
                dma((n_z, HOPS)),
                dma((2 * n_z - 1, n_y - 1, HOPS)),
                dma((n_k, HOPS)),
                dma((n_x - 1, pieces)),
                dma((pieces,)),
                dma((n_x - 1, pieces)),
                dma((n_s, pieces)),
                dma((n_s - 1,)),
                dma((n_s,)),
                dma((chunks,)),
                dma((chunks,)),
                dma((n_x - 1, chunks)),
                dma((n_x - 1, chunks)),
                dma((chunks,)),
                dma((chunks,)),
                dma((n_k - 1,)),
                dma((n_k,)),
                dma((n_y - 1, n_z, PARTS)),
                dma((n_y - 1, n_z, PARTS)),
                dma((n_z - 1, PARTS)),
                dma((n_z - 1, PARTS)),
            ],
            compiler_params=pltpu.CompilerParams(
                collective_id=0, has_side_effects=True, vmem_limit_bytes=56 * 2**20
            ),
            cost_estimate=pl.CostEstimate(
                flops=24 * rows_m * cols * rank,
                bytes_accessed=4 * rows_m * cols,
                transcendentals=2 * rows_m * cols,
            ),
        )(abundance, loadings.T, activity)
        turned, updated = pl.pallas_call(
            hand_over,
            out_shape=(
                jax.ShapeDtypeStruct((width, rows_m), F32),
                jax.ShapeDtypeStruct((rows_h, cols), F32),
            ),
            in_specs=[whole, whole],
            out_specs=(whole, whole),
        )(turned, updated)
        return turned.T, updated

    in_specs = (P("kmer", "samp"), P("kmer", "samp"), P("kmer", "samp"))
    out_specs = (P("kmer", "samp"), P("kmer", "samp"))
    return jax.shard_map(
        per_device, mesh=mesh, in_specs=in_specs, out_specs=out_specs, check_vma=False
    )
```

```python
import functools

import jax
import jax.numpy as jnp
from jax import lax
from jax.experimental import pallas as pl
from jax.experimental.pallas import tpu as pltpu
from jax.sharding import PartitionSpec as P

F32, BF16 = jnp.float32, jnp.bfloat16
LANES = 128
PIECE = 512
PARTS = 2
FLYING = 3
HOPS = 2
TILES = 2
CORES = 2


def halves(value):
    high = value.astype(BF16)
    return high, (value - high.astype(F32)).astype(BF16)


def quotient_of(above, below):
    guess = pl.reciprocal(below, approx=True)
    return above * (guess * (2.0 - below * guess))


def dot(a, b):
    return jnp.dot(a, b, preferred_element_type=F32)


def kernel(
    sizes, ab_hbm, load_ref, act_ref, newload_ref, newact_ref,
    ab, abt, wbuf, w3, hbuf, h3, ht3, tbuf, tsum, nbuf, recv_a, sbuf, recv_x, ubuf, acct, acc, cbuf, csum, column, recv_y, ybuf, recv_z,
    ab_sem, hr_s, hl_s, hy_s, h_r, wx_s, wc_s, wf_s, w_r, t_s, t_r, a_s, a_r, x_s, x_r, u_s, u_r, c_s, c_r,
    ry_s, ry_r, rz_s, rz_r,
):
    n_k, n_s, n_z, n_y, chunk = sizes
    n_x = n_s // CORES
    width, rows_m = load_ref.shape
    rows_h, cols = act_ref.shape
    rank = rows_h * n_k
    pieces = rows_m // PIECE
    chunks = rows_m // chunk
    half = rank // 2

    k, s = lax.axis_index("kmer"), lax.axis_index("samp")
    z, y = lax.div(k, n_y), lax.rem(k, n_y)
    x, core = lax.div(s, CORES), lax.rem(s, CORES)
    mate = x * CORES + (1 - core)

    def z_at(d):
        return lax.rem(z + d, n_z)

    def y_at(d):
        return lax.rem(y + d, n_y)

    def x_at(d):
        return lax.rem(x + d, n_x) * CORES + core

    def put(src, dst, send, recv, kk, ss):
        return pltpu.make_async_remote_copy(
            src_ref=src, dst_ref=dst, send_sem=send, recv_sem=recv,
            device_id={"kmer": kk, "samp": ss}, device_id_type=pl.DeviceIdType.MESH,
        )

    def block(start, size):
        return pl.ds(pl.multiple_of(start, size), size)

    def arrived(dst, sem):
        put(dst, dst, sem, sem, k, mate).wait_recv()

    sent = []

    def go(*args, when=None):
        copy = put(*args)
        sent.append((when, copy))
        if when is None:
            copy.start()
        else:
            pl.when(when)(copy.start)

    def fetch(c):
        rows = pl.ds(c * chunk, chunk)
        return pltpu.make_async_copy(ab_hbm.at[rows, :], ab.at[rows, :], ab_sem.at[c])

    for c in range(chunks):
        fetch(c).start()

    hbuf[block(k * rows_h, rows_h), :] = act_ref[...]
    wbuf[block(s * width, width), :] = load_ref[...]

    barrier = pltpu.get_barrier_semaphore()
    peers = [(lax.rem(k + d, n_k), s) for d in range(1, n_k)]
    peers += [(k, lax.rem(s + d, n_s)) for d in range(1, n_s)]
    for kk, ss in peers:
        pl.semaphore_signal(
            barrier, inc=1, device_id={"kmer": kk, "samp": ss}, device_id_type=pl.DeviceIdType.MESH
        )
    pl.semaphore_wait(barrier, len(peers))

    part_h = cols // HOPS

    def hslot(kk, p):
        return hbuf.at[block(kk * rows_h, rows_h), pl.ds(p * part_h, part_h)]

    def wslot(ss, j):
        return wbuf.at[block(ss * width, width), pl.ds(j * PIECE, PIECE)]

    def pass_h(zz, i, p, when):
        kk = zz * n_y + y
        slot, recv = hslot(kk, p), h_r.at[kk, p]
        up, down = jnp.minimum(z + 1, n_z - 1), jnp.maximum(z - 1, 0)
        if i >= 0:
            ok = z < n_z - 1
            go(slot, slot, hr_s.at[abs(i), p], recv, up * n_y + y, s, when=ok if when is None else ok & when)
        if i <= 0:
            ok = z > 0
            go(slot, slot, hl_s.at[abs(i), p], recv, down * n_y + y, s, when=ok if when is None else ok & when)
        for d in range(1, n_y):
            go(slot, slot, hy_s.at[n_z - 1 + i, d - 1, p], recv, z * n_y + y_at(d), s, when=when)

    for p in range(HOPS):
        pass_h(z, 0, p, None)
    for j in range(pieces):
        for d in range(1, n_x):
            go(wslot(s, j), wslot(s, j), wx_s.at[d - 1, j], w_r.at[s, j], k, x_at(d))
        go(wslot(s, j), wslot(s, j), wc_s.at[j], w_r.at[s, j], k, mate)

    def take_h(i, p):
        there = (z >= i) if i > 0 else (z - i <= n_z - 1)
        zz = jnp.clip(z - i, 0, n_z - 1)
        kk = zz * n_y + y

        @pl.when(there)
        def _():
            arrived(hslot(kk, p), h_r.at[kk, p])

        pass_h(zz, i, p, there)

    def take_w(j):
        for d in range(1, n_x):
            src = x_at(d)
            arrived(wslot(src, j), w_r.at[src, j])
            go(wslot(src, j), wslot(src, j), wf_s.at[d - 1, j], w_r.at[src, j], k, mate)

    waits = max(n_z - 1, pieces)
    turns = pl.cdiv(chunks, waits)
    for i in range(waits):
        if i < n_z - 1:
            for p in range(HOPS):
                take_h(i + 1, p)
                take_h(-i - 1, p)
        if i < pieces:
            take_w(i)
        for c in range(i * turns, min((i + 1) * turns, chunks)):
            fetch(c).wait()
            at = slice(c * chunk, (c + 1) * chunk)
            abt[:, at] = ab[at, :].T

    for j in range(pieces):
        for d in range(n_x):
            src = lax.rem(x + d, n_x) * CORES + (1 - core)
            arrived(wslot(src, j), w_r.at[src, j])
        at = slice(j * PIECE, (j + 1) * PIECE)
        high, low = halves(wbuf[:, at])
        w3[:, at] = jnp.concatenate([high, low, high], axis=0)

    row_totals = jnp.zeros((1, rank), F32)
    for p in range(HOPS):
        for d in range(1, n_y):
            for i in range(n_z):
                src = i * n_y + y_at(d)
                arrived(hslot(src, p), h_r.at[src, p])
        at = slice(p * part_h, (p + 1) * part_h)
        high, low = halves(hbuf[:, at])
        h3[:, at] = jnp.concatenate([high, low], axis=0)
        turned = hbuf[:, at].T
        high, low = halves(turned)
        ht3[at, :] = jnp.concatenate([high, high, low], axis=1)
        row_totals = row_totals + jnp.sum(turned, axis=0, keepdims=True)
    tbuf[s] = jnp.broadcast_to(row_totals, (8, rank))
    for d in range(1, n_s):
        go(tbuf.at[s], tbuf.at[s], t_s.at[d - 1], t_r.at[s], k, lax.rem(s + d, n_s))

    mine = block(core * half, half)

    def out_a(c):
        return put(
            nbuf.at[c, block((1 - core) * half, half), :], recv_a.at[c], a_s.at[c], a_r.at[c], k, mate
        )

    def out_x(c, d):
        return put(sbuf.at[c], recv_x.at[d - 1, c], x_s.at[d - 1, c], x_r.at[d - 1, c], k, x_at(d))

    def out_u(c):
        return put(ubuf.at[c, mine, :], ubuf.at[c, mine, :], u_s.at[c], u_r.at[c], k, mate)

    ahead = max(1, chunks // 2)
    tile = cols // TILES
    tiles = [slice(i * tile, (i + 1) * tile) for i in range(TILES)]

    def scale_rows(c):
        total = sbuf[c]
        for d in range(1, n_x):
            out_x(c, d).wait_recv()
            total = total + recv_x[d - 1, c]
        ubuf[c, mine, :] = wbuf[mine, block(c * chunk, chunk)] * total * tsum[mine, 0:1]
        out_u(c).start()

    def rows_step(c, carry):
        @pl.when(c < chunks)
        def _():
            rows = block(c * chunk, chunk)
            numer = jnp.zeros((rank, chunk), F32)
            for at in tiles:
                high, low = halves(quotient_of(abt[at, rows], dot(ht3[at, :], w3[:, rows])))
                both = dot(h3[:, at], high)
                numer = numer + both[:rank] + both[rank:] + dot(h3[:rank, at], low)
            nbuf[c] = numer
            out_a(c).start()

        @pl.when(c == 1)
        def _():
            for d in range(1, n_s):
                src = lax.rem(s + d, n_s)
                arrived(tbuf.at[src], t_r.at[src])
            totals = tbuf[0]
            for i in range(1, n_s):
                totals = totals + tbuf[i]
            tsum[...] = 1.0 / jnp.broadcast_to(totals[0:1, :], (LANES, rank)).T

        @pl.when(c != 1)
        def _():
            b = jnp.maximum(c - 1, 0)
            out_a(b).wait_recv()
            sbuf[b] = nbuf[b, mine, :] + recv_a[b]
            for d in range(1, n_x):
                out_x(b, d).start()

        @pl.when(c > ahead)
        def _():
            scale_rows(c - 1 - ahead)

        return carry

    lax.fori_loop(0, chunks + 1, rows_step, 0)
    acct[...] = jnp.zeros_like(acct)
    csum[...] = jnp.zeros_like(csum)

    def cols_step(c, carry):
        @pl.when((c < chunks) & (c >= chunks - ahead))
        def _():
            scale_rows(c)

        @pl.when(c >= 1)
        def _():
            b = c - 1
            out_u(b).wait_recv()
            updated = ubuf[b]
            high, low = halves(updated)
            right = jnp.concatenate([high, low, high], axis=0)
            turned = updated.T
            csum[...] += jnp.broadcast_to(jnp.sum(turned, axis=0, keepdims=True), csum.shape)
            high, low = halves(turned)
            left = jnp.concatenate([high, low, high], axis=0)
            for at in tiles:
                rebuilt = dot(ht3[at, :], right)
                q_high, q_low = halves(quotient_of(abt[at, block(b * chunk, chunk)], rebuilt))
                acct[at, :] += dot(jnp.concatenate([q_high, q_high, q_low], axis=1), left)

        return carry

    lax.fori_loop(0, chunks + 1, cols_step, 0)
    acc[...] = acct[...].T

    near = []
    for d in range(1, n_z // 2 + 1):
        near += [d] if d == n_z - d else [d, n_z - d]
    part = cols // PARTS
    steps = [(i, d, p) for i, d in enumerate(near[::-1] + [0]) for p in range(PARTS)]

    def part_of(p):
        return pl.ds(p * part, part)

    def send_y(i, d, p):
        for e in range(1, n_y):
            go(
                acc.at[block((z_at(d) * n_y + y_at(e)) * rows_h, rows_h), part_of(p)],
                recv_y.at[e - 1, i, :, part_of(p)],
                ry_s.at[e - 1, i, p], ry_r.at[e - 1, i, p], z * n_y + y_at(e), s,
            )

    for step in steps[:FLYING]:
        send_y(*step)
    cbuf[k] = csum[...]
    for d in range(1, n_k):
        go(cbuf.at[k], cbuf.at[k], c_s.at[d - 1], c_r.at[k], lax.rem(k + d, n_k), s)
    for c in range(chunks):
        newload_ref[:, c * chunk:(c + 1) * chunk] = ubuf[c, block(s * width, width), :]

    for at, (i, d, p) in enumerate(steps):
        for e in range(1, n_y):
            arrived(recv_y.at[e - 1, i, :, part_of(p)], ry_r.at[e - 1, i, p])
        if at + FLYING < len(steps):
            send_y(*steps[at + FLYING])
        total = acc[block((z_at(d) * n_y + y) * rows_h, rows_h), part_of(p)]
        for e in range(1, n_y):
            total = total + recv_y[e - 1, i, :, part_of(p)]
        ybuf[i, :, part_of(p)] = total
        if d:
            go(
                ybuf.at[i, :, part_of(p)], recv_z.at[i, :, part_of(p)],
                rz_s.at[i, p], rz_r.at[i, p], z_at(d) * n_y + y, s,
            )

    for d in range(1, n_k):
        src = lax.rem(k + d, n_k)
        arrived(cbuf.at[src], c_r.at[src])
    sums = cbuf[0, 0:1, :]
    for i in range(1, n_k):
        sums = sums + cbuf[i, 0:1, :]
    column[...] = jnp.broadcast_to(sums, (LANES, rank)).T
    scaled = act_ref[...] / column[block(k * rows_h, rows_h), 0:1]
    for p in range(PARTS):
        total = ybuf[n_z - 1, :, part_of(p)]
        for i in range(n_z - 1):
            arrived(recv_z.at[i, :, part_of(p)], rz_r.at[i, p])
            total = total + recv_z[i, :, part_of(p)]
        newact_ref[:, part_of(p)] = scaled[:, p * part:(p + 1) * part] * total

    for when, copy in sent:
        if when is None:
            copy.wait_send()
        else:
            pl.when(when)(copy.wait_send)

    def close(c, carry):
        out_a(c).wait_send()
        out_u(c).wait_send()
        for d in range(1, n_x):
            out_x(c, d).wait_send()
        return carry

    lax.fori_loop(0, chunks, close, 0)


def hand_over(load_in, act_in, load_out, act_out):
    load_out[...] = load_in[...]
    act_out[...] = act_in[...]


def solution(mesh):
    n_k, n_s = mesh.shape["kmer"], mesh.shape["samp"]
    n_y = max(d for d in range(1, n_k + 1) if n_k % d == 0 and d * d <= n_k)
    n_z, n_x = n_k // n_y, n_s // CORES

    def per_device(abundance, loadings, activity):
        rows_m, width = loadings.shape
        rows_h, cols = activity.shape
        rank = rows_h * n_k
        chunk = 256
        chunks, pieces = rows_m // chunk, rows_m // PIECE
        vmem, dma = pltpu.VMEM, pltpu.SemaphoreType.DMA
        whole = pl.BlockSpec(memory_space=pltpu.VMEM)
        turned, updated = pl.pallas_call(
            functools.partial(kernel, (n_k, n_s, n_z, n_y, chunk)),
            out_shape=(
                jax.ShapeDtypeStruct((width, rows_m), F32),
                jax.ShapeDtypeStruct((rows_h, cols), F32),
            ),
            in_specs=[pl.BlockSpec(memory_space=pl.ANY), whole, whole],
            out_specs=(whole, whole),
            scratch_shapes=[
                vmem((rows_m, cols), F32),
                vmem((cols, rows_m), F32),
                vmem((rank, rows_m), F32),
                vmem((3 * rank, rows_m), BF16),
                vmem((rank, cols), F32),
                vmem((2 * rank, cols), BF16),
                vmem((cols, 3 * rank), BF16),
                vmem((n_s, 8, rank), F32),
                vmem((rank, LANES), F32),
                vmem((chunks, rank, chunk), F32),
                vmem((chunks, rank // 2, chunk), F32),
                vmem((chunks, rank // 2, chunk), F32),
                vmem((n_x - 1, chunks, rank // 2, chunk), F32),
                vmem((chunks, rank, chunk), F32),
                vmem((cols, rank), F32),
                vmem((rank, cols), F32),
                vmem((n_k, 8, rank), F32),
                vmem((8, rank), F32),
                vmem((rank, LANES), F32),
                vmem((n_y - 1, n_z, rows_h, cols), F32),
                vmem((n_z, rows_h, cols), F32),
                vmem((n_z - 1, rows_h, cols), F32),
                dma((chunks,)),
                dma((n_z, HOPS)),
                dma((n_z, HOPS)),
                dma((2 * n_z - 1, n_y - 1, HOPS)),
                dma((n_k, HOPS)),
                dma((n_x - 1, pieces)),
                dma((pieces,)),
                dma((n_x - 1, pieces)),
                dma((n_s, pieces)),
                dma((n_s - 1,)),
                dma((n_s,)),
                dma((chunks,)),
                dma((chunks,)),
                dma((n_x - 1, chunks)),
                dma((n_x - 1, chunks)),
                dma((chunks,)),
                dma((chunks,)),
                dma((n_k - 1,)),
                dma((n_k,)),
                dma((n_y - 1, n_z, PARTS)),
                dma((n_y - 1, n_z, PARTS)),
                dma((n_z - 1, PARTS)),
                dma((n_z - 1, PARTS)),
            ],
            compiler_params=pltpu.CompilerParams(
                collective_id=0, has_side_effects=True, vmem_limit_bytes=56 * 2**20
            ),
            cost_estimate=pl.CostEstimate(
                flops=24 * rows_m * cols * rank,
                bytes_accessed=4 * rows_m * cols,
                transcendentals=2 * rows_m * cols,
            ),
        )(abundance, loadings.T, activity)
        turned, updated = pl.pallas_call(
            hand_over,
            out_shape=(
                jax.ShapeDtypeStruct((width, rows_m), F32),
                jax.ShapeDtypeStruct((rows_h, cols), F32),
            ),
            in_specs=[whole, whole],
            out_specs=(whole, whole),
        )(turned, updated)
        return turned.T, updated

    in_specs = (P("kmer", "samp"), P("kmer", "samp"), P("kmer", "samp"))
    out_specs = (P("kmer", "samp"), P("kmer", "samp"))
    return jax.shard_map(
        per_device, mesh=mesh, in_specs=in_specs, out_specs=out_specs, check_vma=False
    )
```

```python
import functools

import jax
import jax.numpy as jnp
from jax import lax
from jax.experimental import pallas as pl
from jax.experimental.pallas import tpu as pltpu
from jax.sharding import PartitionSpec as P

F32, BF16 = jnp.float32, jnp.bfloat16
LANES = 128
PIECE = 512
PARTS = 2
FLYING = 3
HOPS = 2
TILES = 4
CORES = 2


def halves(value):
    high = value.astype(BF16)
    return high, (value - high.astype(F32)).astype(BF16)


def quotient_of(above, below):
    guess = pl.reciprocal(below, approx=True)
    return above * (guess * (2.0 - below * guess))


def dot(a, b):
    return jnp.dot(a, b, preferred_element_type=F32)


def kernel(
    sizes, ab_hbm, load_ref, act_ref, newload_ref, newact_ref,
    ab, abt, wbuf, w3, hbuf, h3, ht3, tbuf, tsum, nbuf, recv_a, sbuf, recv_x, ubuf, acct, acc, cbuf, csum, column, recv_y, ybuf, recv_z,
    ab_sem, hr_s, hl_s, hy_s, h_r, wx_s, wc_s, wf_s, w_r, t_s, t_r, a_s, a_r, x_s, x_r, u_s, u_r, c_s, c_r,
    ry_s, ry_r, rz_s, rz_r,
):
    n_k, n_s, n_z, n_y, chunk = sizes
    n_x = n_s // CORES
    width, rows_m = load_ref.shape
    rows_h, cols = act_ref.shape
    rank = rows_h * n_k
    pieces = rows_m // PIECE
    chunks = rows_m // chunk
    half = rank // 2

    k, s = lax.axis_index("kmer"), lax.axis_index("samp")
    z, y = lax.div(k, n_y), lax.rem(k, n_y)
    x, core = lax.div(s, CORES), lax.rem(s, CORES)
    mate = x * CORES + (1 - core)

    def z_at(d):
        return lax.rem(z + d, n_z)

    def y_at(d):
        return lax.rem(y + d, n_y)

    def x_at(d):
        return lax.rem(x + d, n_x) * CORES + core

    def put(src, dst, send, recv, kk, ss):
        return pltpu.make_async_remote_copy(
            src_ref=src, dst_ref=dst, send_sem=send, recv_sem=recv,
            device_id={"kmer": kk, "samp": ss}, device_id_type=pl.DeviceIdType.MESH,
        )

    def block(start, size):
        return pl.ds(pl.multiple_of(start, size), size)

    def arrived(dst, sem):
        put(dst, dst, sem, sem, k, mate).wait_recv()

    sent = []

    def go(*args, when=None):
        copy = put(*args)
        sent.append((when, copy))
        if when is None:
            copy.start()
        else:
            pl.when(when)(copy.start)

    def fetch(c):
        rows = pl.ds(c * chunk, chunk)
        return pltpu.make_async_copy(ab_hbm.at[rows, :], ab.at[rows, :], ab_sem.at[c])

    for c in range(chunks):
        fetch(c).start()

    hbuf[block(k * rows_h, rows_h), :] = act_ref[...]
    wbuf[block(s * width, width), :] = load_ref[...]

    barrier = pltpu.get_barrier_semaphore()
    peers = [(lax.rem(k + d, n_k), s) for d in range(1, n_k)]
    peers += [(k, lax.rem(s + d, n_s)) for d in range(1, n_s)]
    for kk, ss in peers:
        pl.semaphore_signal(
            barrier, inc=1, device_id={"kmer": kk, "samp": ss}, device_id_type=pl.DeviceIdType.MESH
        )
    pl.semaphore_wait(barrier, len(peers))

    part_h = cols // HOPS

    def hslot(kk, p):
        return hbuf.at[block(kk * rows_h, rows_h), pl.ds(p * part_h, part_h)]

    def wslot(ss, j):
        return wbuf.at[block(ss * width, width), pl.ds(j * PIECE, PIECE)]

    def pass_h(zz, i, p, when):
        kk = zz * n_y + y
        slot, recv = hslot(kk, p), h_r.at[kk, p]
        up, down = jnp.minimum(z + 1, n_z - 1), jnp.maximum(z - 1, 0)
        if i >= 0:
            ok = z < n_z - 1
            go(slot, slot, hr_s.at[abs(i), p], recv, up * n_y + y, s, when=ok if when is None else ok & when)
        if i <= 0:
            ok = z > 0
            go(slot, slot, hl_s.at[abs(i), p], recv, down * n_y + y, s, when=ok if when is None else ok & when)
        for d in range(1, n_y):
            go(slot, slot, hy_s.at[n_z - 1 + i, d - 1, p], recv, z * n_y + y_at(d), s, when=when)

    for p in range(HOPS):
        pass_h(z, 0, p, None)
    for j in range(pieces):
        for d in range(1, n_x):
            go(wslot(s, j), wslot(s, j), wx_s.at[d - 1, j], w_r.at[s, j], k, x_at(d))
        go(wslot(s, j), wslot(s, j), wc_s.at[j], w_r.at[s, j], k, mate)

    def take_h(i, p):
        there = (z >= i) if i > 0 else (z - i <= n_z - 1)
        zz = jnp.clip(z - i, 0, n_z - 1)
        kk = zz * n_y + y

        @pl.when(there)
        def _():
            arrived(hslot(kk, p), h_r.at[kk, p])

        pass_h(zz, i, p, there)

    def take_w(j):
        for d in range(1, n_x):
            src = x_at(d)
            arrived(wslot(src, j), w_r.at[src, j])
            go(wslot(src, j), wslot(src, j), wf_s.at[d - 1, j], w_r.at[src, j], k, mate)

    waits = max(n_z - 1, pieces)
    turns = pl.cdiv(chunks, waits)
    for i in range(waits):
        if i < n_z - 1:
            for p in range(HOPS):
                take_h(i + 1, p)
                take_h(-i - 1, p)
        if i < pieces:
            take_w(i)
        for c in range(i * turns, min((i + 1) * turns, chunks)):
            fetch(c).wait()
            at = slice(c * chunk, (c + 1) * chunk)
            abt[:, at] = ab[at, :].T

    for j in range(pieces):
        for d in range(n_x):
            src = lax.rem(x + d, n_x) * CORES + (1 - core)
            arrived(wslot(src, j), w_r.at[src, j])
        at = slice(j * PIECE, (j + 1) * PIECE)
        high, low = halves(wbuf[:, at])
        w3[:, at] = jnp.concatenate([high, low, high], axis=0)

    row_totals = jnp.zeros((1, rank), F32)
    for p in range(HOPS):
        for d in range(1, n_y):
            for i in range(n_z):
                src = i * n_y + y_at(d)
                arrived(hslot(src, p), h_r.at[src, p])
        at = slice(p * part_h, (p + 1) * part_h)
        high, low = halves(hbuf[:, at])
        h3[:, at] = jnp.concatenate([high, low], axis=0)
        turned = hbuf[:, at].T
        high, low = halves(turned)
        ht3[at, :] = jnp.concatenate([high, high, low], axis=1)
        row_totals = row_totals + jnp.sum(turned, axis=0, keepdims=True)
    tbuf[s] = jnp.broadcast_to(row_totals, (8, rank))
    for d in range(1, n_s):
        go(tbuf.at[s], tbuf.at[s], t_s.at[d - 1], t_r.at[s], k, lax.rem(s + d, n_s))

    mine = block(core * half, half)

    def out_a(c):
        return put(
            nbuf.at[c, block((1 - core) * half, half), :], recv_a.at[c], a_s.at[c], a_r.at[c], k, mate
        )

    def out_x(c, d):
        return put(sbuf.at[c], recv_x.at[d - 1, c], x_s.at[d - 1, c], x_r.at[d - 1, c], k, x_at(d))

    def out_u(c):
        return put(ubuf.at[c, mine, :], ubuf.at[c, mine, :], u_s.at[c], u_r.at[c], k, mate)

    ahead = max(1, chunks // 2)
    tile = cols // TILES
    tiles = [slice(i * tile, (i + 1) * tile) for i in range(TILES)]

    def scale_rows(c):
        total = sbuf[c]
        for d in range(1, n_x):
            out_x(c, d).wait_recv()
            total = total + recv_x[d - 1, c]
        ubuf[c, mine, :] = wbuf[mine, block(c * chunk, chunk)] * total * tsum[mine, 0:1]
        out_u(c).start()

    def rows_step(c, carry):
        @pl.when(c < chunks)
        def _():
            rows = block(c * chunk, chunk)
            numer = jnp.zeros((rank, chunk), F32)
            for at in tiles:
                high, low = halves(quotient_of(abt[at, rows], dot(ht3[at, :], w3[:, rows])))
                both = dot(h3[:, at], high)
                numer = numer + both[:rank] + both[rank:] + dot(h3[:rank, at], low)
            nbuf[c] = numer
            out_a(c).start()

        @pl.when(c == 1)
        def _():
            for d in range(1, n_s):
                src = lax.rem(s + d, n_s)
                arrived(tbuf.at[src], t_r.at[src])
            totals = tbuf[0]
            for i in range(1, n_s):
                totals = totals + tbuf[i]
            tsum[...] = 1.0 / jnp.broadcast_to(totals[0:1, :], (LANES, rank)).T

        @pl.when(c != 1)
        def _():
            b = jnp.maximum(c - 1, 0)
            out_a(b).wait_recv()
            sbuf[b] = nbuf[b, mine, :] + recv_a[b]
            for d in range(1, n_x):
                out_x(b, d).start()

        @pl.when(c > ahead)
        def _():
            scale_rows(c - 1 - ahead)

        return carry

    lax.fori_loop(0, chunks + 1, rows_step, 0)
    acct[...] = jnp.zeros_like(acct)
    csum[...] = jnp.zeros_like(csum)

    def cols_step(c, carry):
        @pl.when((c < chunks) & (c >= chunks - ahead))
        def _():
            scale_rows(c)

        @pl.when(c >= 1)
        def _():
            b = c - 1
            out_u(b).wait_recv()
            updated = ubuf[b]
            high, low = halves(updated)
            right = jnp.concatenate([high, low, high], axis=0)
            turned = updated.T
            csum[...] += jnp.broadcast_to(jnp.sum(turned, axis=0, keepdims=True), csum.shape)
            high, low = halves(turned)
            left = jnp.concatenate([high, low, high], axis=0)
            for at in tiles:
                rebuilt = dot(ht3[at, :], right)
                q_high, q_low = halves(quotient_of(abt[at, block(b * chunk, chunk)], rebuilt))
                acct[at, :] += dot(jnp.concatenate([q_high, q_high, q_low], axis=1), left)

        return carry

    lax.fori_loop(0, chunks + 1, cols_step, 0)
    acc[...] = acct[...].T

    near = []
    for d in range(1, n_z // 2 + 1):
        near += [d] if d == n_z - d else [d, n_z - d]
    part = cols // PARTS
    steps = [(i, d, p) for i, d in enumerate(near[::-1] + [0]) for p in range(PARTS)]

    def part_of(p):
        return pl.ds(p * part, part)

    def send_y(i, d, p):
        for e in range(1, n_y):
            go(
                acc.at[block((z_at(d) * n_y + y_at(e)) * rows_h, rows_h), part_of(p)],
                recv_y.at[e - 1, i, :, part_of(p)],
                ry_s.at[e - 1, i, p], ry_r.at[e - 1, i, p], z * n_y + y_at(e), s,
            )

    for step in steps[:FLYING]:
        send_y(*step)
    cbuf[k] = csum[...]
    for d in range(1, n_k):
        go(cbuf.at[k], cbuf.at[k], c_s.at[d - 1], c_r.at[k], lax.rem(k + d, n_k), s)
    for c in range(chunks):
        newload_ref[:, c * chunk:(c + 1) * chunk] = ubuf[c, block(s * width, width), :]

    for at, (i, d, p) in enumerate(steps):
        for e in range(1, n_y):
            arrived(recv_y.at[e - 1, i, :, part_of(p)], ry_r.at[e - 1, i, p])
        if at + FLYING < len(steps):
            send_y(*steps[at + FLYING])
        total = acc[block((z_at(d) * n_y + y) * rows_h, rows_h), part_of(p)]
        for e in range(1, n_y):
            total = total + recv_y[e - 1, i, :, part_of(p)]
        ybuf[i, :, part_of(p)] = total
        if d:
            go(
                ybuf.at[i, :, part_of(p)], recv_z.at[i, :, part_of(p)],
                rz_s.at[i, p], rz_r.at[i, p], z_at(d) * n_y + y, s,
            )

    for d in range(1, n_k):
        src = lax.rem(k + d, n_k)
        arrived(cbuf.at[src], c_r.at[src])
    sums = cbuf[0, 0:1, :]
    for i in range(1, n_k):
        sums = sums + cbuf[i, 0:1, :]
    column[...] = jnp.broadcast_to(sums, (LANES, rank)).T
    scaled = act_ref[...] / column[block(k * rows_h, rows_h), 0:1]
    for p in range(PARTS):
        total = ybuf[n_z - 1, :, part_of(p)]
        for i in range(n_z - 1):
            arrived(recv_z.at[i, :, part_of(p)], rz_r.at[i, p])
            total = total + recv_z[i, :, part_of(p)]
        newact_ref[:, part_of(p)] = scaled[:, p * part:(p + 1) * part] * total

    for when, copy in sent:
        if when is None:
            copy.wait_send()
        else:
            pl.when(when)(copy.wait_send)

    def close(c, carry):
        out_a(c).wait_send()
        out_u(c).wait_send()
        for d in range(1, n_x):
            out_x(c, d).wait_send()
        return carry

    lax.fori_loop(0, chunks, close, 0)


def hand_over(load_in, act_in, load_out, act_out):
    load_out[...] = load_in[...]
    act_out[...] = act_in[...]


def solution(mesh):
    n_k, n_s = mesh.shape["kmer"], mesh.shape["samp"]
    n_y = max(d for d in range(1, n_k + 1) if n_k % d == 0 and d * d <= n_k)
    n_z, n_x = n_k // n_y, n_s // CORES

    def per_device(abundance, loadings, activity):
        rows_m, width = loadings.shape
        rows_h, cols = activity.shape
        rank = rows_h * n_k
        chunk = 256
        chunks, pieces = rows_m // chunk, rows_m // PIECE
        vmem, dma = pltpu.VMEM, pltpu.SemaphoreType.DMA
        whole = pl.BlockSpec(memory_space=pltpu.VMEM)
        turned, updated = pl.pallas_call(
            functools.partial(kernel, (n_k, n_s, n_z, n_y, chunk)),
            out_shape=(
                jax.ShapeDtypeStruct((width, rows_m), F32),
                jax.ShapeDtypeStruct((rows_h, cols), F32),
            ),
            in_specs=[pl.BlockSpec(memory_space=pl.ANY), whole, whole],
            out_specs=(whole, whole),
            scratch_shapes=[
                vmem((rows_m, cols), F32),
                vmem((cols, rows_m), F32),
                vmem((rank, rows_m), F32),
                vmem((3 * rank, rows_m), BF16),
                vmem((rank, cols), F32),
                vmem((2 * rank, cols), BF16),
                vmem((cols, 3 * rank), BF16),
                vmem((n_s, 8, rank), F32),
                vmem((rank, LANES), F32),
                vmem((chunks, rank, chunk), F32),
                vmem((chunks, rank // 2, chunk), F32),
                vmem((chunks, rank // 2, chunk), F32),
                vmem((n_x - 1, chunks, rank // 2, chunk), F32),
                vmem((chunks, rank, chunk), F32),
                vmem((cols, rank), F32),
                vmem((rank, cols), F32),
                vmem((n_k, 8, rank), F32),
                vmem((8, rank), F32),
                vmem((rank, LANES), F32),
                vmem((n_y - 1, n_z, rows_h, cols), F32),
                vmem((n_z, rows_h, cols), F32),
                vmem((n_z - 1, rows_h, cols), F32),
                dma((chunks,)),
                dma((n_z, HOPS)),
                dma((n_z, HOPS)),
                dma((2 * n_z - 1, n_y - 1, HOPS)),
                dma((n_k, HOPS)),
                dma((n_x - 1, pieces)),
                dma((pieces,)),
                dma((n_x - 1, pieces)),
                dma((n_s, pieces)),
                dma((n_s - 1,)),
                dma((n_s,)),
                dma((chunks,)),
                dma((chunks,)),
                dma((n_x - 1, chunks)),
                dma((n_x - 1, chunks)),
                dma((chunks,)),
                dma((chunks,)),
                dma((n_k - 1,)),
                dma((n_k,)),
                dma((n_y - 1, n_z, PARTS)),
                dma((n_y - 1, n_z, PARTS)),
                dma((n_z - 1, PARTS)),
                dma((n_z - 1, PARTS)),
            ],
            compiler_params=pltpu.CompilerParams(
                collective_id=0, has_side_effects=True, vmem_limit_bytes=56 * 2**20
            ),
            cost_estimate=pl.CostEstimate(
                flops=24 * rows_m * cols * rank,
                bytes_accessed=4 * rows_m * cols,
                transcendentals=2 * rows_m * cols,
            ),
        )(abundance, loadings.T, activity)
        turned, updated = pl.pallas_call(
            hand_over,
            out_shape=(
                jax.ShapeDtypeStruct((width, rows_m), F32),
                jax.ShapeDtypeStruct((rows_h, cols), F32),
            ),
            in_specs=[whole, whole],
            out_specs=(whole, whole),
        )(turned, updated)
        return turned.T, updated

    in_specs = (P("kmer", "samp"), P("kmer", "samp"), P("kmer", "samp"))
    out_specs = (P("kmer", "samp"), P("kmer", "samp"))
    return jax.shard_map(
        per_device, mesh=mesh, in_specs=in_specs, out_specs=out_specs, check_vma=False
    )
```
